128 devices in a mesh: gx: 8 (over z, core), gy: 16 (over y, x).
Axes of the slice: x: 4, y: 4, z: 4, core: 2. Of those that a mesh axis runs over, the one named last changes fastest.
Arguments:
- positions: float32 [3, 64, 128, 256], P(None, 'gx', 'gy'), may hold values from 0 to 1
- charges: float32 [64, 128, 256], P('gx', 'gy'), may hold values from -0.3 to 0.3
- counts: int32 [64, 128, 8], P('gx', 'gy'), may hold values from 8 to 32, as said below
- compress: float32 [512, 128], replicated, may hold values from -0.25 to 0.25
- operators: float32 [316, 128, 128], replicated, may hold values from -0.1875 to 0.1875
- expand: float32 [128, 512], replicated, may hold values from -2 to 2
Outputs:
- potential: float32 [64, 128, 256], P('gx', 'gy')
The draws below stay inside these ranges and needn't reach their ends.
Inputs may be any that keep to these rules, and one draw needn't show every extreme that they name: `counts`: some leaf holds exactly 32 particles in every draw.
All inputs are finite; a program needn't handle non-finite values.
Results may differ from the reference program's by a relative error of at most 0.00011.
Values sent between devices are 32-bit elements; how exact they have to be, the bound alone decides.
No kernel may reach another device: no remote copies, remote signals or barrier semaphores. Data moves between devices by JAX's collectives and lax.ppermute only.
A program may use at most 448 MiB of HBM per device.

```python
import jax
import jax.numpy as jnp
from jax import lax

ORDER = 8
COEF = 512
RANK = 128
OFFSETS = 316
BLOCK = 8
SLOTS = 32
LEAVES_X = 64
LEAVES_Y = 128


def draw_counts(key, part):
    drawn = jax.random.randint(key, (LEAVES_X * LEAVES_Y * BLOCK,), SLOTS // 4, SLOTS + 1, dtype=jnp.int32)
    chosen = jax.random.randint(jax.random.fold_in(key, 11), (), 0, LEAVES_X * LEAVES_Y * BLOCK, dtype=jnp.int32)
    filled = jnp.where(jnp.arange(LEAVES_X * LEAVES_Y * BLOCK, dtype=jnp.int32) == chosen, SLOTS, drawn)
    return filled.reshape(LEAVES_X, LEAVES_Y, BLOCK)


def block_scale(key, dims, cuts, low, high):
    level, own = 1.0, jax.random.fold_in(key, 6)
    for position, parts in cuts:
        draws = jnp.exp(jax.random.uniform(jax.random.fold_in(own, position), (parts,), jnp.float32, low / len(cuts), high / len(cuts)))
        level = level * jnp.repeat(draws, dims[position] // parts).reshape([-1 if axis == position else 1 for axis in range(len(dims))])
    return level


def noise(own_key, dims, spread, reach, shards=(), kind=jnp.bfloat16):
    result = jax.random.normal(own_key, dims, jnp.float32) * spread
    if len(shards) > 0:
        result = block_scale(own_key, dims, shards, -0.22, 0.18) * result
    return jnp.clip(result, min=-reach, max=reach).astype(kind)


def setup_inputs(seed: int = 0) -> dict:
    seeds = jax.random.split(jax.random.key(seed), 7)
    return {
        "positions": jnp.clip(1.0 * jax.random.uniform(seeds[0], (3, LEAVES_X, LEAVES_Y, BLOCK * SLOTS), jnp.float32) ** block_scale(seeds[0], (3, LEAVES_X, LEAVES_Y, BLOCK * SLOTS), ((1, 8), (2, 16)), -0.2, 0.2), 0.0, 1.0),
        "charges": noise(seeds[1], (LEAVES_X, LEAVES_Y, BLOCK * SLOTS), 0.05, 0.3, ((0, 8), (1, 16)), jnp.float32),
        "counts": draw_counts(jax.random.fold_in(seeds[6], 71), 0),
        "compress": noise(seeds[3], (COEF, RANK), COEF ** -0.5, 0.25, (), jnp.float32),
        "operators": noise(seeds[4], (OFFSETS, RANK, RANK), (8 * RANK) ** -0.5, 0.1875, (), jnp.float32),
        "expand": noise(seeds[5], (RANK, COEF), (max(RANK // 16, 1)) ** -0.5, 2.0, (), jnp.float32),
    }


PRECISE = lax.Precision.HIGHEST
SOFTENING = 0.01

def cheb_weights(points, degree):
    angles = jnp.pi * (2.0 * jnp.arange(degree, dtype=jnp.float32) + 1.0) / (2.0 * degree)
    harmonic = jnp.arange(1, degree, dtype=jnp.float32)
    phases = jnp.arccos(jnp.clip(points, -1.0, 1.0))
    series = jnp.cos(harmonic[:, None] * phases[None, :])
    node_series = jnp.cos(harmonic[:, None] * angles[None, :])
    return 1.0 / degree + 2.0 / degree * jnp.dot(node_series.T, series, precision=PRECISE)

def transfer_matrix(degree):
    angles = jnp.pi * (2.0 * jnp.arange(degree, dtype=jnp.float32) + 1.0) / (2.0 * degree)
    node_points = jnp.cos(angles)
    child_sides = jnp.array([-1.0, 1.0], dtype=jnp.float32)
    shifted = 0.5 * (node_points[None, :] + child_sides[:, None])
    factor = cheb_weights(shifted.reshape(-1), degree).reshape(degree, 2, degree).transpose(1, 2, 0)
    product = factor[:, None, None, :, None, None, :, None, None] * factor[None, :, None, None, :, None, None, :, None] * factor[None, None, :, None, None, :, None, None, :]
    return product.reshape(8 * degree ** 3, degree ** 3)

def upward(children, transfer):
    side_x, side_y, side_z, columns = children.shape
    grouped = children.reshape(side_x // 2, 2, side_y // 2, 2, side_z // 2, 2, columns).transpose(0, 2, 4, 1, 3, 5, 6)
    flattened = grouped.reshape(side_x // 2 * (side_y // 2) * (side_z // 2), 8 * columns)
    return jnp.dot(flattened, transfer, precision=PRECISE).reshape(side_x // 2, side_y // 2, side_z // 2, columns)

def downward(parent, transfer):
    side_x, side_y, side_z, columns = parent.shape
    flattened = jnp.dot(parent.reshape(side_x * side_y * side_z, columns), transfer.T, precision=PRECISE)
    grouped = flattened.reshape(side_x, side_y, side_z, 2, 2, 2, columns).transpose(0, 3, 1, 4, 2, 5, 6)
    return grouped.reshape(2 * side_x, 2 * side_y, 2 * side_z, columns)

def full_operators(operators):
    reduced = operators.shape[-1]
    pieces = []
    cursor = 0
    for offset_x in range(7):
        for offset_y in range(7):
            if abs(offset_x - 3) <= 1 and abs(offset_y - 3) <= 1:
                pieces.append(operators[cursor:cursor + 2])
                pieces.append(jnp.zeros((3, reduced, reduced), operators.dtype))
                pieces.append(operators[cursor + 2:cursor + 4])
                cursor += 4
            else:
                pieces.append(operators[cursor:cursor + 7])
                cursor += 7
    return jnp.concatenate(pieces, 0).reshape(7, 7, 7, reduced, reduced)

def windows(padded, count_x, count_y, count_z):
    interior = padded[1:-1, 1:-1, 1:-1]
    reduced = interior.shape[-1]
    paired = interior.reshape(count_x + 2, 2, count_y + 2, 2, count_z + 2, 2, reduced)
    along_x = jnp.stack([paired[lag_index:lag_index + count_x] for lag_index in range(3)], axis=1)
    along_y = jnp.stack([along_x[:, :, :, lag_index:lag_index + count_y] for lag_index in range(3)], axis=4)
    along_z = jnp.stack([along_y[:, :, :, :, :, :, lag_index:lag_index + count_z] for lag_index in range(3)], axis=7)
    ordered = along_z.transpose(0, 3, 6, 1, 2, 4, 5, 7, 8, 9)
    return ordered.reshape(count_x * count_y * count_z, 216 * reduced)

def translate(sources, operator_grid):
    reduced = operator_grid.shape[-1]
    outputs = []
    for parity in range(8):
        parity_x = parity // 4
        parity_y = parity // 2 % 2
        parity_z = parity % 2
        operator_block = operator_grid[1 - parity_x:7 - parity_x, 1 - parity_y:7 - parity_y, 1 - parity_z:7 - parity_z]
        outputs.append(jnp.dot(sources, operator_block.reshape(216 * reduced, reduced), precision=PRECISE))
    return jnp.stack(outputs, 0)

def spread_children(children_parts, count_x, count_y, count_z):
    reduced = children_parts.shape[-1]
    grouped = children_parts.reshape(2, 2, 2, count_x, count_y, count_z, reduced).transpose(3, 0, 4, 1, 5, 2, 6)
    return grouped.reshape(2 * count_x, 2 * count_y, 2 * count_z, reduced)

def particle_basis(points, slot_count):
    unrolled = 2.0 * points.reshape(3, -1) - 1.0
    return [cheb_weights(unrolled[component], ORDER).reshape(ORDER, -1, slot_count) for component in range(3)]

def leaf_multipoles(points, weighted, slot_count):
    basis_x, basis_y, basis_z = particle_basis(points, slot_count)
    masses = weighted.reshape(-1, slot_count)
    moments = jnp.einsum('ls,als,bls,gls->labg', masses, basis_x, basis_y, basis_z, precision=PRECISE)
    return moments.reshape(masses.shape[0], ORDER ** 3)

def far_field(points, expansions, slot_count):
    basis_x, basis_y, basis_z = particle_basis(points, slot_count)
    shaped = expansions.reshape(-1, ORDER, ORDER, ORDER)
    return jnp.einsum('labg,als,bls,gls->ls', shaped, basis_x, basis_y, basis_z, precision=PRECISE)

def near_field(padded, count_x, count_y, count_z):
    slot_count = padded.shape[-1]
    centre = padded[:, 1:1 + count_x, 1:1 + count_y, 1:1 + count_z]
    others = 1.0 - jnp.eye(slot_count, dtype=padded.dtype)
    summed = jnp.zeros(centre.shape[1:], padded.dtype)
    for shift_x in (-1, 0, 1):
        for shift_y in (-1, 0, 1):
            for shift_z in (-1, 0, 1):
                source = padded[:, 1 + shift_x:1 + shift_x + count_x, 1 + shift_y:1 + shift_y + count_y, 1 + shift_z:1 + shift_z + count_z]
                squared = None
                for component, offset in ((0, shift_x), (1, shift_y), (2, shift_z)):
                    spacing = centre[component][..., :, None] - source[component][..., None, :] - offset
                    squared = spacing * spacing if squared is None else squared + spacing * spacing
                kernel = source[3][..., None, :] * lax.rsqrt(squared + SOFTENING)
                if shift_x == 0 and shift_y == 0 and (shift_z == 0):
                    kernel = kernel * others
                summed = summed + lax.optimization_barrier(jnp.sum(kernel, axis=-1))
    return summed

def reduce_grid(grid_values, compress):
    shape_head = grid_values.shape[:3]
    return jnp.dot(grid_values.reshape(-1, COEF), compress, precision=PRECISE).reshape(shape_head + (compress.shape[1],))

def expand_grid(grid_values, expand):
    shape_head = grid_values.shape[:3]
    return jnp.dot(grid_values.reshape(-1, expand.shape[0]), expand, precision=PRECISE).reshape(shape_head + (COEF,))

def level_locals(coarse, level_scale, operator_grid):
    count_x = coarse.shape[0] // 2
    count_y = coarse.shape[1] // 2
    count_z = coarse.shape[2] // 2
    padded = jnp.pad(coarse, ((3, 3), (3, 3), (3, 3), (0, 0)))

    def one_slab(slab_index):
        window = lax.dynamic_slice_in_dim(padded, 2 * slab_index, 8, 0)
        source_rows = windows(window, 1, count_y, count_z)
        return spread_children(translate(source_rows, operator_grid), 1, count_y, count_z)
    slab_parts = lax.map(one_slab, jnp.arange(count_x, dtype=jnp.int32))
    return slab_parts.reshape(2 * count_x, 2 * count_y, 2 * count_z, coarse.shape[3]) * level_scale

def reference(positions, charges, counts, compress, operators, expand):
    slot_count = SLOTS
    occupied = jnp.arange(slot_count, dtype=jnp.int32)[None, None, None, :] < counts[..., None]
    occupied = occupied.astype(jnp.float32).reshape(LEAVES_X, LEAVES_Y, BLOCK * slot_count)
    weighted = charges * occupied
    transfer = transfer_matrix(ORDER)
    row_points = jnp.moveaxis(positions, 1, 0)

    def leaf_row(pair):
        return leaf_multipoles(pair[0][:, None], pair[1][None], slot_count)
    leaf_m = lax.map(leaf_row, (row_points, weighted)).reshape(LEAVES_X, LEAVES_Y, BLOCK, COEF)
    parent_m = upward(leaf_m, transfer)
    grand_m = upward(parent_m, transfer)
    operator_grid = full_operators(operators)
    leaf_lc = level_locals(reduce_grid(leaf_m, compress), 1.0, operator_grid)
    parent_lc = level_locals(reduce_grid(parent_m, compress), 0.5, operator_grid)
    grand_lc = level_locals(reduce_grid(grand_m, compress), 0.25, operator_grid)
    grand_l = expand_grid(grand_lc, expand)
    parent_l = expand_grid(parent_lc, expand) + downward(grand_l, transfer)
    leaf_l = expand_grid(leaf_lc, expand) + downward(parent_l, transfer)

    def far_row(pair):
        return far_field(pair[0][:, None], pair[1].reshape(-1, COEF), slot_count)
    far_part = lax.map(far_row, (row_points, leaf_l)).reshape(LEAVES_X, LEAVES_Y, BLOCK * slot_count)
    stacked = jnp.concatenate([positions, weighted[None]], 0).reshape(4, LEAVES_X, LEAVES_Y, BLOCK, slot_count)
    padded = jnp.pad(stacked, ((0, 0), (1, 1), (1, 1), (1, 1), (0, 0)))

    def near_row(slab_index):
        slab = lax.dynamic_slice_in_dim(padded, slab_index, 3, 1)
        return near_field(slab, 1, LEAVES_Y, BLOCK)
    near_part = lax.map(near_row, jnp.arange(LEAVES_X, dtype=jnp.int32)).reshape(LEAVES_X, LEAVES_Y, BLOCK * slot_count)
    return (far_part + near_part) * occupied
```

```python
import math

import jax
import jax.numpy as jnp
import numpy as np
from jax import lax
from jax.experimental import pallas as pl
from jax.experimental.pallas import tpu as pltpu
from jax.sharding import PartitionSpec as P

F32 = jnp.float32
BF16 = jnp.bfloat16
SOFTENING = 0.01
EXACT = lax.Precision.HIGHEST

FACE = 232
CORNER = 64
PACKED = FACE + 2 * CORNER
FACE_PAR, FACE_GRAND, FACE_NEAR = 128, 160, 168
COR_PAR, COR_GRAND, COR_NEAR = 32, 48, 56


def node_cos():
    return np.array(
        [[math.cos(math.pi * k * (2 * a + 1) / 16) for a in range(8)] for k in range(8)]
    )


def cheb_numpy(points):
    series = np.cos(np.arange(1, 8)[:, None] * np.arccos(points)[None, :])
    return 1 / 8 + 2 / 8 * node_cos()[1:].T @ series


def transfer_factor():
    nodes = np.cos(np.pi * (2 * np.arange(8) + 1) / 16)
    points = 0.5 * (nodes[None, :] + np.array([-1.0, 1.0])[:, None])
    weights = cheb_numpy(points.reshape(-1)).reshape(8, 2, 8)
    return weights.transpose(1, 2, 0)


def make_constants():
    factor = transfer_factor()
    lane = np.arange(128)
    lane_z, lane_x, lane_y = lane // 64, lane // 8 % 8, lane % 8
    lanes = np.zeros((4, 64, 128))
    for level in range(2):
        for which, coordinate in ((0, lane_x), (1, lane_y)):
            side = coordinate >> level & 1
            lanes[2 * level + which] = factor[side].transpose(1, 2, 0).reshape(64, 128)
    up_z = np.zeros((16, 8, 2, 16, 8))
    for block in range(16):
        for side in range(2):
            up_z[block, :, side, block, :] = factor[side].T
    up_z = up_z.reshape(128, 256)
    pick_par = np.zeros((64, 256))
    for x in range(4):
        for y in range(4):
            for z in range(4):
                pick_par[(x * 4 + y) * 4 + z, z % 2 * 128 + z // 2 * 64 + 2 * x * 8 + 2 * y] = 1
    pick_grand = np.zeros((8, 128))
    for x in range(2):
        for y in range(2):
            for z in range(2):
                pick_grand[(x * 2 + y) * 2 + z, z * 64 + 4 * x * 8 + 4 * y] = 1
    spread = np.kron(np.eye(8), np.ones((1, 32)))

    near_row = {}
    for x in range(8):
        for y in range(8):
            near_row[x, y] = x * 8 + y
    for y in range(8):
        near_row[-1, y] = 64 + y
        near_row[8, y] = 72 + y
        near_row[y, -1] = 80 + y
        near_row[y, 8] = 88 + y
    near_row[-1, -1], near_row[8, -1], near_row[-1, 8], near_row[8, 8] = 96, 97, 98, 99
    near_pick = np.zeros((256, 9, 128))
    for k in range(9):
        dx, dy = k // 3 - 1, k % 3 - 1
        for ln in range(128):
            row = near_row[int(lane_x[ln]) + dx, int(lane_y[ln]) + dy]
            near_pick[lane_z[ln] * 128 + row, k, ln] = 1
    near_pick = near_pick.reshape(256, 1152)

    leaf_row = {}
    for x in range(8):
        for y in range(8):
            leaf_row[x, y] = x * 8 + y
    for i in range(2):
        for y in range(8):
            leaf_row[i - 2, y] = 64 + i * 8 + y
            leaf_row[8 + i, y] = 80 + i * 8 + y
            leaf_row[y, i - 2] = 96 + y * 2 + i
            leaf_row[y, 8 + i] = 112 + y * 2 + i
        for j in range(2):
            leaf_row[i - 2, j - 2] = 128 + i * 2 + j
            leaf_row[8 + i, j - 2] = 136 + i * 2 + j
            leaf_row[i - 2, 8 + j] = 144 + i * 2 + j
            leaf_row[8 + i, 8 + j] = 152 + i * 2 + j
    leaf_pick = np.zeros((36, 16, 256))
    for v in range(36):
        sx, sy = v // 6 - 2, v % 6 - 2
        for r in range(16):
            leaf_pick[v, r, leaf_row[2 * (r // 4) + sx, 2 * (r % 4) + sy]] = 1
    leaf_pick = leaf_pick.reshape(576, 256)

    par_row = {}
    for x in range(4):
        for y in range(4):
            par_row[x, y] = x * 4 + y
    for i in range(2):
        for y in range(4):
            par_row[i - 2, y] = 16 + i * 4 + y
            par_row[4 + i, y] = 24 + i * 4 + y
            par_row[y, i - 2] = 32 + y * 2 + i
            par_row[y, 4 + i] = 40 + y * 2 + i
        for j in range(2):
            par_row[i - 2, j - 2] = 48 + i * 2 + j
            par_row[4 + i, j - 2] = 52 + i * 2 + j
            par_row[i - 2, 4 + j] = 56 + i * 2 + j
            par_row[4 + i, 4 + j] = 60 + i * 2 + j
    grand_row = {}
    order = [(0, 0), (-2, 0), (2, 0), (0, -2), (0, 2), (-2, -2), (2, -2), (-2, 2), (2, 2)]
    for n, (ox, oy) in enumerate(order):
        for i in range(2):
            for j in range(2):
                grand_row[ox + i, oy + j] = 128 + n * 4 + i * 2 + j
    small_pick = np.zeros((36, 3, 16, 256))
    for v in range(36):
        sx, sy = v // 6 - 2, v % 6 - 2
        for d in range(3):
            for r in range(8):
                zp = r // 4 + d - 1
                if 0 <= zp < 2:
                    row = par_row[2 * (r // 2 % 2) + sx, 2 * (r % 2) + sy]
                    small_pick[v, d, r, zp * 64 + row] = 1
            if d == 1:
                small_pick[v, d, 8, grand_row[sx, sy]] = 1
    small_pick = small_pick.reshape(1728, 256)

    place_leaf = np.zeros((128, 128))
    for z in range(2):
        for px in range(2):
            for py in range(2):
                for xp in range(4):
                    for yp in range(4):
                        row = ((z * 2 + px) * 2 + py) * 16 + xp * 4 + yp
                        place_leaf[row, z * 64 + (2 * xp + px) * 8 + 2 * yp + py] = 1
    place_small = np.zeros((3, 128, 128))
    for ln in range(128):
        z, x, y = int(lane_z[ln]), int(lane_x[ln]) >> 1, int(lane_y[ln]) >> 1
        for q in range(2):
            row = (((q * 2 + z) * 2 + x % 2) * 2 + y % 2) * 4 + x // 2 * 2 + y // 2
            place_small[q, row, ln] = 1
        place_small[2, 64 + ((x >> 1) * 2 + (y >> 1)) * 2 + z, ln] = 1

    def half(array):
        return np.asarray(array, np.float32).astype(jnp.bfloat16)

    return dict(
        lanes=np.asarray(lanes, np.float32),
        up_z=np.asarray(up_z, np.float32),
        down_z=np.asarray(up_z.T, np.float32),
        pick_par=np.asarray(pick_par, np.float32),
        pick_grand=np.asarray(pick_grand, np.float32),
        spread=half(spread),
        near_pick=half(near_pick),
        leaf_pick=half(leaf_pick),
        small_pick=half(small_pick),
        place_leaf=half(place_leaf),
        place_small=half(place_small),
    )


def mm(a, b):
    return jnp.dot(a, b, preferred_element_type=F32)


def split2(x):
    high = x.astype(BF16)
    return high, (x - high.astype(F32)).astype(BF16)


def split3(x):
    high = x.astype(BF16)
    rest = x - high.astype(F32)
    mid = rest.astype(BF16)
    return high, mid, (rest - mid.astype(F32)).astype(BF16)


def mm3(a, b):
    a_high, a_low = a
    b_high, b_low = b
    return mm(a_high, b_high) + (mm(a_high, b_low) + mm(a_low, b_high))


def lanes_first(block):
    return jnp.concatenate([block[:, :128], block[:, 128:]], axis=0).T


def basis(points):
    u = jnp.clip(2.0 * points - 1.0, -1.0, 1.0)
    series = [None, u]
    for _ in range(2, 8):
        before = series[-2] if len(series) > 2 else 1.0
        series.append(2.0 * u * series[-1] - before)
    table = node_cos()
    weights = [None] * 8
    for a in range(4):
        even = 0.125
        odd = None
        for k in range(1, 8):
            term = series[k] * np.float32(0.25 * table[k, a])
            if k % 2 == 0:
                even = even + term
            else:
                odd = term if odd is None else odd + term
        weights[a] = even + odd
        weights[7 - a] = even - odd
    return weights


def occupied_slots(counts_ref, spread_ref):
    limits = mm(counts_ref[...].astype(F32).astype(BF16), spread_ref[...])
    slot = lax.broadcasted_iota(jnp.int32, (64, 256), 1) & 31
    return jnp.where(slot.astype(F32) < limits, 1.0, 0.0)


def bcast(ref, row):
    return jnp.broadcast_to(ref[pl.ds(row, 1), :], (8, 128))


def mix_x(source, target, lanes_ref, which, up):
    for out in range(8):
        total = None
        for inner in range(8):
            row = inner * 8 + out if up else out * 8 + inner
            term = lanes_ref[which, row : row + 1, :] * source[inner * 64 : inner * 64 + 64, :]
            total = term if total is None else total + term
        if up:
            shift = 8 << (which // 2)
            total = total + pltpu.roll(total, 128 - shift, 1)
        target[out * 64 : out * 64 + 64, :] = total


def mix_y(source, target, lanes_ref, which, up):
    def one(a, carry):
        start = pl.multiple_of(a * 64, 64)
        rows = [source[pl.ds(start + 8 * b, 8), :] for b in range(8)]
        for out in range(8):
            total = None
            for inner in range(8):
                row = inner * 8 + out if up else out * 8 + inner
                term = lanes_ref[which, row : row + 1, :] * rows[inner]
                total = term if total is None else total + term
            if up:
                shift = 1 << (which // 2)
                total = total + pltpu.roll(total, 128 - shift, 1)
            target[pl.ds(start + 8 * out, 8), :] = total
        return carry

    lax.fori_loop(0, 8, one, 0)


def upward_kernel(
    pos, charges, counts, compress, lanes, up_z, pick_par, pick_grand, spread,
    leaf, par, grand, xs_low, xs_high, ys_low, ys_high, weighted,
    flat, basis_x, basis_y, basis_z, moments, work_a, work_b, parents,
):
    w = charges[...] * occupied_slots(counts, spread)
    weighted[...] = w
    for component in range(3):
        flat[component] = lanes_first(pos[component])
    flat[3] = lanes_first(w)

    def chunk(c, carry):
        rows = pl.ds(pl.multiple_of(c * 32, 32), 32)
        mass = flat[3, rows, :]
        for a, value in enumerate(basis(flat[0, rows, :])):
            basis_x[a * 32 : a * 32 + 32, :] = value
        for a, value in enumerate(basis(flat[1, rows, :])):
            basis_y[a * 32 : a * 32 + 32, :] = value * mass
        for a, value in enumerate(basis(flat[2, rows, :])):
            basis_z[pl.ds(a, 32, stride=8), :] = value
        for half in range(2):

            def slot(s, sums):
                along_z = basis_z[pl.ds(pl.multiple_of(s * 8, 8), 8), :]
                along_y = [bcast(basis_y, b * 32 + s) for b in range(8)]
                result = []
                for a in range(4):
                    part = bcast(basis_x, (half * 4 + a) * 32 + s) * along_z
                    for b in range(8):
                        result.append(sums[a * 8 + b] + part * along_y[b])
                return tuple(result)

            zero = jnp.zeros((8, 128), F32)
            sums = lax.fori_loop(0, 32, slot, (zero,) * 32)
            for n in range(32):
                moments[c, (half * 32 + n) * 8 : (half * 32 + n) * 8 + 8, :] = sums[n]
        return carry

    lax.fori_loop(0, 4, chunk, 0)
    compress_t = split2(compress[...].T)
    for c in range(4):
        small = mm3(compress_t, split2(moments[c])).T
        for z in range(2):
            leaf[pl.ds(c + 4 * z, 64, stride=8), :] = small[z * 64 : z * 64 + 64, :]

    step = split2(up_z[...])

    def join_z(low, high, target):
        for block in range(4):
            rows = slice(block * 128, block * 128 + 128)
            pair = jnp.concatenate([low[rows, :], high[rows, :]], axis=0)
            target[rows, :] = mm3(step, split2(pair))

    rough = []
    for q in range(2):
        join_z(moments.at[2 * q], moments.at[2 * q + 1], work_a)
        mix_x(work_a, work_b, lanes, 0, True)
        mix_y(work_b, parents.at[q], lanes, 1, True)
        rough.append(mm3(compress_t, split2(parents[q])).T)
    par[...] = jnp.dot(
        pick_par[...], jnp.concatenate(rough, axis=0), precision=EXACT, preferred_element_type=F32
    )
    join_z(parents.at[0], parents.at[1], work_a)
    mix_x(work_a, work_b, lanes, 2, True)
    mix_y(work_b, work_a, lanes, 3, True)
    rough = mm3(compress_t, split2(work_a[...])).T
    grand[...] = jnp.dot(pick_grand[...], rough, precision=EXACT, preferred_element_type=F32)

    def particle(component, cells, part):
        columns = slice(part * 128, part * 128 + 128)
        if component < 3:
            return pos[component, cells, columns]
        return weighted[cells, columns]

    for buffer, x0, px0, xn in ((xs_low, 0, 0, 0), (xs_high, 6, 2, 7)):
        buffer[0:128, :] = leaf[x0 * 64 : x0 * 64 + 128, :]
        buffer[FACE_PAR : FACE_PAR + 32, :] = par[px0 * 16 : px0 * 16 + 32, :]
        buffer[FACE_GRAND : FACE_GRAND + 8, :] = grand[...]
        for corner, y0, py0, yn in ((FACE, 0, 0, 0), (FACE + CORNER, 6, 2, 7)):
            for i in range(2):
                source = ((x0 + i) * 8 + y0) * 8
                buffer[corner + i * 16 : corner + i * 16 + 16, :] = leaf[source : source + 16, :]
                source = ((px0 + i) * 4 + py0) * 4
                target = corner + COR_PAR + i * 8
                buffer[target : target + 8, :] = par[source : source + 8, :]
            target = corner + COR_GRAND
            buffer[target : target + 8, :] = grand[...]
        for component in range(4):
            for part in range(2):
                row = 2 * component + part
                value = particle(component, slice(xn * 8, xn * 8 + 8), part)
                buffer[pl.ds(FACE_NEAR + row, 8, stride=8), :] = value
                for corner, yn in ((FACE, 0), (FACE + CORNER, 7)):
                    target = corner + COR_NEAR + row
                    buffer[target : target + 1, :] = value[yn : yn + 1, :]
    for buffer, y0, py0, yn in ((ys_low, 0, 0, 0), (ys_high, 6, 2, 7)):
        for x in range(8):
            source = (x * 8 + y0) * 8
            buffer[x * 16 : x * 16 + 16, :] = leaf[source : source + 16, :]
        for x in range(4):
            source = (x * 4 + py0) * 4
            target = FACE_PAR + x * 8
            buffer[target : target + 8, :] = par[source : source + 8, :]
        buffer[FACE_GRAND : FACE_GRAND + 8, :] = grand[...]
        for x in range(8):
            for component in range(4):
                for part in range(2):
                    value = particle(component, slice(x * 8 + yn, x * 8 + yn + 1), part)
                    target = FACE_NEAR + x * 8 + 2 * component + part
                    buffer[target : target + 1, :] = value


def near_kernel(
    pos, weighted, x_low, x_high, y_low, y_high, pick, near,
    columns, sources, squares, targets,
):
    columns[...] = jnp.zeros_like(columns)
    for component in range(4):
        for part in range(2):
            row = 2 * component + part
            lanes = slice(part * 128, part * 128 + 128)
            own = pos[component, :, lanes] if component < 3 else weighted[:, lanes]
            columns[row, 0:64, :] = own
            for n, buffer in enumerate((x_low, x_high, y_low, y_high)):
                columns[row, 64 + 8 * n : 72 + 8 * n, :] = buffer[
                    pl.ds(FACE_NEAR + row, 8, stride=8), :
                ]
            for n, buffer in enumerate((y_low, y_high)):
                for side in range(2):
                    source = FACE + side * CORNER + COR_NEAR + row
                    target = 96 + 2 * n + side
                    columns[row, target : target + 1, :] = buffer[source : source + 1, :]
    empty = jnp.zeros((32, 128), F32)
    for component in range(4):
        low = columns[2 * component].T
        high = columns[2 * component + 1].T
        left = jnp.concatenate([empty, low, high[0:32, :]], axis=0)
        right = jnp.concatenate([low[96:128, :], high, empty], axis=0)
        pieces = split3(jnp.concatenate([left, right], axis=1))
        for k in range(9):
            table = pick[:, k * 128 : k * 128 + 128]
            value = (mm(pieces[0], table) + mm(pieces[1], table)) + mm(pieces[2], table)
            if component == 3:
                sources[3, k] = value
                continue
            offset = (k // 3 - 1, k % 3 - 1, 0)[component] - 0.5
            value = value + offset
            if k == 4:
                targets[component] = value[32:160, :]
            sources[component, k] = -2.0 * value
            if component == 0:
                squares[k] = value * value + SOFTENING
            else:
                squares[k] = squares[k] + value * value

    slot = lax.broadcasted_iota(jnp.int32, (8, 128), 0)

    def chunk(c, carry):
        start = pl.multiple_of(c * 32, 32)
        groups = [
            [targets[component, pl.ds(start + 8 * g, 8), :] for component in range(3)]
            for g in range(4)
        ]
        flat = [t[0] * t[0] + t[1] * t[1] for t in groups]
        sums = (jnp.zeros((8, 128), F32),) * 4
        for dz in (-1, 0, 1):
            base = start + 32 * (1 + dz)
            high = [t[2] - float(dz) for t in groups]
            square = [f + h * h for f, h in zip(flat, high)]

            def block(k, sums, own, base=base, high=high, square=square):
                sums = list(sums)
                for s in range(32):
                    row = pl.ds(base + s, 1)
                    px = jnp.broadcast_to(sources[0, k, row, :], (8, 128))
                    py = jnp.broadcast_to(sources[1, k, row, :], (8, 128))
                    pz = jnp.broadcast_to(sources[2, k, row, :], (8, 128))
                    pw = jnp.broadcast_to(sources[3, k, row, :], (8, 128))
                    pq = jnp.broadcast_to(squares[k, row, :], (8, 128))
                    for g in range(4):
                        distance = (
                            (square[g] + pq)
                            + groups[g][0] * px
                            + (groups[g][1] * py + high[g] * pz)
                        )
                        term = pw * lax.rsqrt(distance)
                        if own and s // 8 == g:
                            term = jnp.where(slot == s % 8, 0.0, term)
                        sums[g] = sums[g] + term
                return tuple(sums)

            if dz == 0:
                sums = lax.fori_loop(
                    0, 8, lambda n, t: block(n + jnp.where(n >= 4, 1, 0), t, False), sums
                )
                sums = block(4, sums, True)
            else:
                sums = lax.fori_loop(0, 9, lambda n, t: block(n, t, False), sums)
        for g in range(4):
            near[pl.ds(start + 8 * g, 8), :] = sums[g]
        return carry

    lax.fori_loop(0, 4, chunk, 0)


ROW_STARTS = (0, 49, 98, 138, 178, 218, 267, 316)


def downward_kernel(
    pos, counts, near, leaf, par, grand, x_low, x_high, y_low, y_high, operators, expand,
    lanes, down_z, spread, leaf_pick, small_pick, place_leaf, place_small,
    out,
    weights, staged, small, leaf_high, leaf_low, small_high, small_low, right_high, right_low,
    sums, flat, basis_x, basis_y, basis_z, local, work_a, work_b, work_c, far, arrivals,
):
    copies = [
        pltpu.make_async_copy(
            operators.at[pl.ds(ROW_STARTS[n], ROW_STARTS[n + 1] - ROW_STARTS[n])],
            weights.at[pl.ds(ROW_STARTS[n], ROW_STARTS[n + 1] - ROW_STARTS[n])],
            arrivals.at[n],
        )
        for n in range(7)
    ]
    for copy in copies:
        copy.start()

    staged[...] = jnp.zeros_like(staged)
    small[...] = jnp.zeros_like(small)
    faces = (x_low, x_high, y_low, y_high)
    for z in range(8):
        columns = slice(z * 128, z * 128 + 128)
        staged[0:64, columns] = leaf[pl.ds(z, 64, stride=8), :]
        for n, buffer in enumerate(faces):
            target = 64 + 16 * n
            staged[target : target + 16, columns] = buffer[pl.ds(z, 16, stride=8), :]
        for n, buffer in enumerate((y_low, y_high)):
            for side in range(2):
                target = 128 + 16 * n + 8 * side
                source = FACE + side * CORNER + z
                staged[target : target + 4, columns] = buffer[pl.ds(source, 4, stride=8), :]
    for z in range(4):
        columns = slice(z % 2 * 128, z % 2 * 128 + 128)
        top = z // 2 * 64
        small[top : top + 16, columns] = par[pl.ds(z, 16, stride=4), :]
        for n, buffer in enumerate(faces):
            target = top + 16 + 8 * n
            small[target : target + 8, columns] = buffer[pl.ds(FACE_PAR + z, 8, stride=4), :]
        for n, buffer in enumerate((y_low, y_high)):
            for side in range(2):
                target = top + 48 + 8 * n + 4 * side
                source = FACE + side * CORNER + COR_PAR + z
                small[target : target + 4, columns] = buffer[pl.ds(source, 4, stride=4), :]
    for z in range(2):
        columns = slice(z * 128, z * 128 + 128)
        small[128:132, columns] = grand[pl.ds(z, 4, stride=2), :]
        for n, buffer in enumerate(faces):
            target = 132 + 4 * n
            small[target : target + 4, columns] = buffer[pl.ds(FACE_GRAND + z, 4, stride=2), :]
        for n, buffer in enumerate((y_low, y_high)):
            for side in range(2):
                target = 148 + 8 * n + 4 * side
                source = FACE + side * CORNER + COR_GRAND + z
                small[target : target + 4, columns] = buffer[pl.ds(source, 4, stride=2), :]

    blank = jnp.zeros((36, 16, 256), BF16)
    for target in (leaf_high, leaf_low):
        target[:, 0] = blank
        target[:, 5] = blank
    for zp in range(4):
        pieces = split2(staged[:, zp * 256 : zp * 256 + 256])
        for piece, target in zip(pieces, (leaf_high, leaf_low)):
            target[:, zp + 1] = mm(leaf_pick[...], piece).astype(BF16).reshape(36, 16, 256)
    for piece, target in zip(split2(small[...]), (small_high, small_low)):
        target[...] = mm(small_pick[...], piece).astype(BF16).reshape(36, 3, 16, 256)

    sums[...] = jnp.zeros_like(sums)

    def left(high, v, d):
        main, rest = (leaf_high, small_high) if high else (leaf_low, small_low)
        return jnp.concatenate(
            [main[v, pl.ds(d, 4)].reshape(64, 256), rest[v, d]], axis=0
        )

    def translate(dx, dy, xs, ys, base, beside):
        split = {}
        for n, dz in enumerate((-3, -2, 2, 3) if beside else range(-3, 4)):
            split[dz] = split2(weights[base + n])
        for d in range(3):
            for which, target in ((0, right_high), (1, right_low)):
                for source in range(2):
                    for side in range(2):
                        dz = 2 * (d - 1) + source - side
                        value = split[dz][which] if dz in split else jnp.zeros((128, 128), BF16)
                        target[
                            d,
                            source * 128 : source * 128 + 128,
                            side * 128 : side * 128 + 128,
                        ] = value
        total = None
        sides = [(px, py) for px in xs for py in ys]
        for d in range(3):
            if beside and d == 1:
                continue
            variants = [(px + dx + 2) * 6 + (py + dy + 2) for px, py in sides]
            upper = jnp.concatenate([left(True, v, d) for v in variants], axis=0)
            lower = jnp.concatenate([left(False, v, d) for v in variants], axis=0)
            term = (mm(upper, right_high[d]) + mm(lower, right_high[d])) + mm(upper, right_low[d])
            total = term if total is None else total + term
        for n, (px, py) in enumerate(sides):
            sums[px * 2 + py] = sums[px * 2 + py] + total[n * 80 : n * 80 + 80, :]

    both = (0, 1)
    for n, dx in enumerate(range(-3, 4)):
        copies[n].wait()
        start = ROW_STARTS[n]
        xs = (1,) if dx == -3 else (0,) if dx == 3 else both
        middle = abs(dx) <= 1
        translate(dx, -3, xs, (1,), start, False)
        if middle:
            translate(dx, -2, xs, both, start + 7, False)
            lax.fori_loop(
                0,
                3,
                lambda i, t: (translate(dx, i - 1, xs, both, start + 14 + 4 * i, True), t)[1],
                0,
            )
            translate(dx, 2, xs, both, start + 26, False)
            translate(dx, 3, xs, (0,), start + 33, False)
        else:
            lax.fori_loop(
                0,
                5,
                lambda i, t: (translate(dx, i - 2, xs, both, start + 7 + 7 * i, False), t)[1],
                0,
            )
            translate(dx, 3, xs, (0,), start + 42, False)

    grow = split2(expand[...].T)
    pairs = [(px, py) for px in both for py in both]

    def expanded(rows, place):
        flipped = split2(rows.T)
        placed = tuple(mm(piece, place).astype(BF16) for piece in flipped)
        return mm3(grow, placed)

    pieces = []
    for q in range(2):
        for z in range(2):
            for px, py in pairs:
                rows = slice(64 + 4 * z, 68 + 4 * z)
                pieces.append(sums[px * 2 + py, rows, q * 128 : q * 128 + 128] * 0.5)
    for px, py in pairs:
        for z in range(2):
            pieces.append(sums[px * 2 + py, 72:73, z * 128 : z * 128 + 128] * 0.25)
    pieces.append(jnp.zeros((56, 128), F32))
    coarse = jnp.concatenate(pieces, axis=0)
    step = split2(down_z[...])

    work_a[...] = expanded(coarse, place_small[2])
    mix_x(work_a, work_b, lanes, 2, False)
    mix_y(work_b, work_c, lanes, 3, False)

    for component in range(3):
        flat[component] = lanes_first(pos[component])

    for q in range(2):
        side = tuple(piece[q * 128 : q * 128 + 128, :] for piece in step)
        work_a[...] = expanded(coarse, place_small[q])
        for block in range(4):
            rows = slice(block * 128, block * 128 + 128)
            work_a[rows, :] = work_a[rows, :] + mm3(side, split2(work_c[rows, :]))
        mix_x(work_a, work_b, lanes, 0, False)
        mix_y(work_b, work_a, lanes, 1, False)
        for cz in range(2):
            rows = [
                sums[px * 2 + py, (q + 2 * z) * 16 : (q + 2 * z) * 16 + 16, cz * 128 : cz * 128 + 128]
                for z in range(2)
                for px, py in pairs
            ]
            side = tuple(piece[cz * 128 : cz * 128 + 128, :] for piece in step)
            local[2 * q + cz] = expanded(jnp.concatenate(rows, axis=0), place_leaf[...])
            for block in range(4):
                part = slice(block * 128, block * 128 + 128)
                local[2 * q + cz, part, :] = local[2 * q + cz, part, :] + mm3(
                    side, split2(work_a[part, :])
                )

    def chunk(c, carry):
        start = pl.multiple_of(c * 32, 32)
        rows = pl.ds(start, 32)
        for a, value in enumerate(basis(flat[0, rows, :])):
            basis_x[a * 32 : a * 32 + 32, :] = value
        for a, value in enumerate(basis(flat[1, rows, :])):
            basis_y[a * 32 : a * 32 + 32, :] = value
        for a, value in enumerate(basis(flat[2, rows, :])):
            basis_z[pl.ds(a, 32, stride=8), :] = value

        def slots(n, carry):
            first = 2 * n
            totals = [None, None]
            along_y = [[bcast(basis_y, b * 32 + first + j) for b in range(8)] for j in range(2)]
            for a in range(8):
                inner = [None, None]
                for b in range(8):
                    value = local[c, (a * 8 + b) * 8 : (a * 8 + b) * 8 + 8, :]
                    for j in range(2):
                        term = value * along_y[j][b]
                        inner[j] = term if inner[j] is None else inner[j] + term
                for j in range(2):
                    term = inner[j] * bcast(basis_x, a * 32 + first + j)
                    totals[j] = term if totals[j] is None else totals[j] + term
            for j in range(2):
                along_z = basis_z[pl.ds(pl.multiple_of((first + j) * 8, 8), 8), :]
                far[pl.ds(start + first + j, 1), :] = jnp.sum(
                    totals[j] * along_z, axis=0, keepdims=True
                )
            return carry

        lax.fori_loop(0, 16, slots, 0)
        return carry

    lax.fori_loop(0, 4, chunk, 0)
    total = (far[...] + near[...]).T
    occupied = occupied_slots(counts, spread)
    out[...] = jnp.concatenate([total[0:64, :], total[64:128, :]], axis=1) * occupied


def vmem(count):
    return [pl.BlockSpec(memory_space=pltpu.VMEM) for _ in range(count)]


def shaped(*dims):
    return jax.ShapeDtypeStruct(dims, F32)


def neighbours(low, high, axis):
    count = lax.axis_size(axis)
    up = [(i, i + 1) for i in range(count - 1)]
    down = [(target, source) for source, target in up]
    return lax.ppermute(high, axis, up), lax.ppermute(low, axis, down)


def per_device(positions, charges, counts, compress, operators, expand):
    const = {name: jnp.asarray(value) for name, value in make_constants().items()}
    pos = positions.reshape(3, 64, 256)
    cells = counts.reshape(64, 8)
    limit = pltpu.CompilerParams(vmem_limit_bytes=56 * 1024 * 1024)
    leaf, par, grand, xs_low, xs_high, ys_low, ys_high, weighted = pl.pallas_call(
        upward_kernel,
        out_shape=[
            shaped(512, 128), shaped(64, 128), shaped(8, 128),
            shaped(PACKED, 128), shaped(PACKED, 128), shaped(FACE, 128), shaped(FACE, 128),
            shaped(64, 256),
        ],
        in_specs=vmem(9),
        out_specs=vmem(8),
        scratch_shapes=[
            pltpu.VMEM((4, 128, 128), F32),
            pltpu.VMEM((256, 128), F32),
            pltpu.VMEM((256, 128), F32),
            pltpu.VMEM((256, 128), F32),
            pltpu.VMEM((4, 512, 128), F32),
            pltpu.VMEM((512, 128), F32),
            pltpu.VMEM((512, 128), F32),
            pltpu.VMEM((2, 512, 128), F32),
        ],
        compiler_params=limit,
        name="upward",
    )(
        pos, charges.reshape(64, 256), cells, compress, const["lanes"], const["up_z"],
        const["pick_par"], const["pick_grand"], const["spread"],
    )
    x_low, x_high = neighbours(xs_low, xs_high, "gx")
    first, second = slice(FACE, FACE + CORNER), slice(FACE + CORNER, PACKED)
    y_low, y_high = neighbours(
        jnp.concatenate([ys_low, x_low[first], x_high[first]], axis=0),
        jnp.concatenate([ys_high, x_low[second], x_high[second]], axis=0),
        "gy",
    )
    near = pl.pallas_call(
        near_kernel,
        out_shape=shaped(128, 128),
        in_specs=vmem(7),
        out_specs=vmem(1)[0],
        scratch_shapes=[
            pltpu.VMEM((8, 128, 128), F32),
            pltpu.VMEM((4, 9, 192, 128), F32),
            pltpu.VMEM((9, 192, 128), F32),
            pltpu.VMEM((3, 128, 128), F32),
        ],
        compiler_params=limit,
        name="near",
    )(pos, weighted, x_low, x_high, y_low, y_high, const["near_pick"])
    result = pl.pallas_call(
        downward_kernel,
        out_shape=shaped(64, 256),
        in_specs=vmem(10) + [pl.BlockSpec(memory_space=pl.ANY)] + vmem(8),
        out_specs=vmem(1)[0],
        scratch_shapes=[
            pltpu.VMEM((316, 128, 128), F32),
            pltpu.VMEM((256, 1024), F32),
            pltpu.VMEM((256, 256), F32),
            pltpu.VMEM((36, 6, 16, 256), BF16),
            pltpu.VMEM((36, 6, 16, 256), BF16),
            pltpu.VMEM((36, 3, 16, 256), BF16),
            pltpu.VMEM((36, 3, 16, 256), BF16),
            pltpu.VMEM((3, 256, 256), BF16),
            pltpu.VMEM((3, 256, 256), BF16),
            pltpu.VMEM((4, 80, 256), F32),
            pltpu.VMEM((3, 128, 128), F32),
            pltpu.VMEM((256, 128), F32),
            pltpu.VMEM((256, 128), F32),
            pltpu.VMEM((256, 128), F32),
            pltpu.VMEM((4, 512, 128), F32),
            pltpu.VMEM((512, 128), F32),
            pltpu.VMEM((512, 128), F32),
            pltpu.VMEM((512, 128), F32),
            pltpu.VMEM((128, 128), F32),
            pltpu.SemaphoreType.DMA((7,)),
        ],
        compiler_params=limit,
        name="downward",
    )(
        pos, cells, near, leaf, par, grand, x_low, x_high, y_low, y_high, operators, expand,
        const["lanes"], const["down_z"], const["spread"], const["leaf_pick"],
        const["small_pick"], const["place_leaf"], const["place_small"],
    )
    return result.reshape(8, 8, 256)


def solution(mesh):
    placed = (P(None, "gx", "gy", None), P("gx", "gy", None), P("gx", "gy", None), P(), P(), P())
    return jax.shard_map(
        per_device, mesh=mesh, in_specs=placed, out_specs=P("gx", "gy", None), check_vma=False
    )
```

```python
import math

import jax
import jax.numpy as jnp
import numpy as np
from jax import lax
from jax.experimental import pallas as pl
from jax.experimental.pallas import tpu as pltpu
from jax.sharding import PartitionSpec as P

F32 = jnp.float32
BF16 = jnp.bfloat16
SOFTENING = 0.01
EXACT = lax.Precision.HIGHEST

FACE = 232
CORNER = 64
PACKED = FACE + 2 * CORNER
FACE_PAR, FACE_GRAND, FACE_NEAR = 128, 160, 168
COR_PAR, COR_GRAND, COR_NEAR = 32, 48, 56


def node_cos():
    return np.array(
        [[math.cos(math.pi * k * (2 * a + 1) / 16) for a in range(8)] for k in range(8)]
    )


def cheb_numpy(points):
    series = np.cos(np.arange(1, 8)[:, None] * np.arccos(points)[None, :])
    return 1 / 8 + 2 / 8 * node_cos()[1:].T @ series


def transfer_factor():
    nodes = np.cos(np.pi * (2 * np.arange(8) + 1) / 16)
    points = 0.5 * (nodes[None, :] + np.array([-1.0, 1.0])[:, None])
    weights = cheb_numpy(points.reshape(-1)).reshape(8, 2, 8)
    return weights.transpose(1, 2, 0)


def make_constants():
    factor = transfer_factor()
    lane = np.arange(128)
    lane_z, lane_x, lane_y = lane // 64, lane // 8 % 8, lane % 8
    lanes = np.zeros((4, 64, 128))
    for level in range(2):
        for which, coordinate in ((0, lane_x), (1, lane_y)):
            side = coordinate >> level & 1
            lanes[2 * level + which] = factor[side].transpose(1, 2, 0).reshape(64, 128)
    up_z = np.zeros((16, 8, 2, 16, 8))
    for block in range(16):
        for side in range(2):
            up_z[block, :, side, block, :] = factor[side].T
    up_z = up_z.reshape(128, 256)
    pick_par = np.zeros((64, 256))
    for x in range(4):
        for y in range(4):
            for z in range(4):
                pick_par[(x * 4 + y) * 4 + z, z % 2 * 128 + z // 2 * 64 + 2 * x * 8 + 2 * y] = 1
    pick_grand = np.zeros((8, 128))
    for x in range(2):
        for y in range(2):
            for z in range(2):
                pick_grand[(x * 2 + y) * 2 + z, z * 64 + 4 * x * 8 + 4 * y] = 1
    spread = np.kron(np.eye(8), np.ones((1, 32)))

    near_row = {}
    for x in range(8):
        for y in range(8):
            near_row[x, y] = x * 8 + y
    for y in range(8):
        near_row[-1, y] = 64 + y
        near_row[8, y] = 72 + y
        near_row[y, -1] = 80 + y
        near_row[y, 8] = 88 + y
    near_row[-1, -1], near_row[8, -1], near_row[-1, 8], near_row[8, 8] = 96, 97, 98, 99
    near_pick = np.zeros((256, 9, 128))
    for k in range(9):
        dx, dy = k // 3 - 1, k % 3 - 1
        for ln in range(128):
            row = near_row[int(lane_x[ln]) + dx, int(lane_y[ln]) + dy]
            near_pick[lane_z[ln] * 128 + row, k, ln] = 1
    near_pick = near_pick.reshape(256, 1152)

    leaf_row = {}
    for x in range(8):
        for y in range(8):
            leaf_row[x, y] = x * 8 + y
    for i in range(2):
        for y in range(8):
            leaf_row[i - 2, y] = 64 + i * 8 + y
            leaf_row[8 + i, y] = 80 + i * 8 + y
            leaf_row[y, i - 2] = 96 + y * 2 + i
            leaf_row[y, 8 + i] = 112 + y * 2 + i
        for j in range(2):
            leaf_row[i - 2, j - 2] = 128 + i * 2 + j
            leaf_row[8 + i, j - 2] = 136 + i * 2 + j
            leaf_row[i - 2, 8 + j] = 144 + i * 2 + j
            leaf_row[8 + i, 8 + j] = 152 + i * 2 + j
    leaf_pick = np.zeros((36, 16, 256))
    for v in range(36):
        sx, sy = v // 6 - 2, v % 6 - 2
        for r in range(16):
            leaf_pick[v, r, leaf_row[2 * (r // 4) + sx, 2 * (r % 4) + sy]] = 1
    leaf_pick = leaf_pick.reshape(576, 256)

    par_row = {}
    for x in range(4):
        for y in range(4):
            par_row[x, y] = x * 4 + y
    for i in range(2):
        for y in range(4):
            par_row[i - 2, y] = 16 + i * 4 + y
            par_row[4 + i, y] = 24 + i * 4 + y
            par_row[y, i - 2] = 32 + y * 2 + i
            par_row[y, 4 + i] = 40 + y * 2 + i
        for j in range(2):
            par_row[i - 2, j - 2] = 48 + i * 2 + j
            par_row[4 + i, j - 2] = 52 + i * 2 + j
            par_row[i - 2, 4 + j] = 56 + i * 2 + j
            par_row[4 + i, 4 + j] = 60 + i * 2 + j
    grand_row = {}
    order = [(0, 0), (-2, 0), (2, 0), (0, -2), (0, 2), (-2, -2), (2, -2), (-2, 2), (2, 2)]
    for n, (ox, oy) in enumerate(order):
        for i in range(2):
            for j in range(2):
                grand_row[ox + i, oy + j] = 128 + n * 4 + i * 2 + j
    small_pick = np.zeros((36, 3, 16, 256))
    for v in range(36):
        sx, sy = v // 6 - 2, v % 6 - 2
        for d in range(3):
            for r in range(8):
                zp = r // 4 + d - 1
                if 0 <= zp < 2:
                    row = par_row[2 * (r // 2 % 2) + sx, 2 * (r % 2) + sy]
                    small_pick[v, d, r, zp * 64 + row] = 1
            if d == 1:
                small_pick[v, d, 8, grand_row[sx, sy]] = 1
    small_pick = small_pick.reshape(1728, 256)

    place_leaf = np.zeros((128, 128))
    for z in range(2):
        for px in range(2):
            for py in range(2):
                for xp in range(4):
                    for yp in range(4):
                        row = ((z * 2 + px) * 2 + py) * 16 + xp * 4 + yp
                        place_leaf[row, z * 64 + (2 * xp + px) * 8 + 2 * yp + py] = 1
    place_small = np.zeros((3, 128, 128))
    for ln in range(128):
        z, x, y = int(lane_z[ln]), int(lane_x[ln]) >> 1, int(lane_y[ln]) >> 1
        for q in range(2):
            row = (((q * 2 + z) * 2 + x % 2) * 2 + y % 2) * 4 + x // 2 * 2 + y // 2
            place_small[q, row, ln] = 1
        place_small[2, 64 + ((x >> 1) * 2 + (y >> 1)) * 2 + z, ln] = 1

    def half(array):
        return np.asarray(array, np.float32).astype(jnp.bfloat16)

    return dict(
        lanes=np.asarray(lanes, np.float32),
        up_z=np.asarray(up_z, np.float32),
        down_z=np.asarray(up_z.T, np.float32),
        pick_par=np.asarray(pick_par, np.float32),
        pick_grand=np.asarray(pick_grand, np.float32),
        spread=half(spread),
        near_pick=half(near_pick),
        leaf_pick=half(leaf_pick),
        small_pick=half(small_pick),
        place_leaf=half(place_leaf),
        place_small=half(place_small),
    )


def mm(a, b):
    return jnp.dot(a, b, preferred_element_type=F32)


def split2(x):
    high = x.astype(BF16)
    return high, (x - high.astype(F32)).astype(BF16)


def split3(x):
    high = x.astype(BF16)
    rest = x - high.astype(F32)
    mid = rest.astype(BF16)
    return high, mid, (rest - mid.astype(F32)).astype(BF16)


def mm3(a, b):
    a_high, a_low = a
    b_high, b_low = b
    return mm(a_high, b_high) + (mm(a_high, b_low) + mm(a_low, b_high))


def lanes_first(block):
    return jnp.concatenate([block[:, :128], block[:, 128:]], axis=0).T


def basis(points):
    u = jnp.clip(2.0 * points - 1.0, -1.0, 1.0)
    series = [None, u]
    for _ in range(2, 8):
        before = series[-2] if len(series) > 2 else 1.0
        series.append(2.0 * u * series[-1] - before)
    table = node_cos()
    weights = [None] * 8
    for a in range(4):
        even = 0.125
        odd = None
        for k in range(1, 8):
            term = series[k] * np.float32(0.25 * table[k, a])
            if k % 2 == 0:
                even = even + term
            else:
                odd = term if odd is None else odd + term
        weights[a] = even + odd
        weights[7 - a] = even - odd
    return weights


def occupied_slots(counts_ref, spread_ref):
    limits = mm(counts_ref[...].astype(F32).astype(BF16), spread_ref[...])
    slot = lax.broadcasted_iota(jnp.int32, (64, 256), 1) & 31
    return jnp.where(slot.astype(F32) < limits, 1.0, 0.0)


def bcast(ref, row):
    return jnp.broadcast_to(ref[pl.ds(row, 1), :], (8, 128))


def mix_x(source, target, lanes_ref, which, up):
    for out in range(8):
        total = None
        for inner in range(8):
            row = inner * 8 + out if up else out * 8 + inner
            term = lanes_ref[which, row : row + 1, :] * source[inner * 64 : inner * 64 + 64, :]
            total = term if total is None else total + term
        if up:
            shift = 8 << (which // 2)
            total = total + pltpu.roll(total, 128 - shift, 1)
        target[out * 64 : out * 64 + 64, :] = total


def mix_y(source, target, lanes_ref, which, up):
    def one(a, carry):
        start = pl.multiple_of(a * 64, 64)
        rows = [source[pl.ds(start + 8 * b, 8), :] for b in range(8)]
        for out in range(8):
            total = None
            for inner in range(8):
                row = inner * 8 + out if up else out * 8 + inner
                term = lanes_ref[which, row : row + 1, :] * rows[inner]
                total = term if total is None else total + term
            if up:
                shift = 1 << (which // 2)
                total = total + pltpu.roll(total, 128 - shift, 1)
            target[pl.ds(start + 8 * out, 8), :] = total
        return carry

    lax.fori_loop(0, 8, one, 0)


def upward_kernel(
    pos, charges, counts, compress, lanes, up_z, pick_par, pick_grand, spread,
    leaf, par, grand, xs_low, xs_high, ys_low, ys_high, weighted,
    flat, basis_x, basis_y, basis_z, moments, work_a, work_b, parents,
):
    w = charges[...] * occupied_slots(counts, spread)
    weighted[...] = w
    for component in range(3):
        flat[component] = lanes_first(pos[component])
    flat[3] = lanes_first(w)

    def chunk(c, carry):
        rows = pl.ds(pl.multiple_of(c * 32, 32), 32)
        mass = flat[3, rows, :]
        for a, value in enumerate(basis(flat[0, rows, :])):
            basis_x[a * 32 : a * 32 + 32, :] = value
        for a, value in enumerate(basis(flat[1, rows, :])):
            basis_y[a * 32 : a * 32 + 32, :] = value * mass
        for a, value in enumerate(basis(flat[2, rows, :])):
            basis_z[pl.ds(a, 32, stride=8), :] = value
        for half in range(2):

            def slot(s, sums):
                along_z = basis_z[pl.ds(pl.multiple_of(s * 8, 8), 8), :]
                along_y = [bcast(basis_y, b * 32 + s) for b in range(8)]
                result = []
                for a in range(4):
                    part = bcast(basis_x, (half * 4 + a) * 32 + s) * along_z
                    for b in range(8):
                        result.append(sums[a * 8 + b] + part * along_y[b])
                return tuple(result)

            zero = jnp.zeros((8, 128), F32)
            sums = lax.fori_loop(0, 32, slot, (zero,) * 32, unroll=4)
            for n in range(32):
                moments[c, (half * 32 + n) * 8 : (half * 32 + n) * 8 + 8, :] = sums[n]
        return carry

    lax.fori_loop(0, 4, chunk, 0)
    compress_t = split2(compress[...].T)
    for c in range(4):
        small = mm3(compress_t, split2(moments[c])).T
        for z in range(2):
            leaf[pl.ds(c + 4 * z, 64, stride=8), :] = small[z * 64 : z * 64 + 64, :]

    step = split2(up_z[...])

    def join_z(low, high, target):
        for block in range(4):
            rows = slice(block * 128, block * 128 + 128)
            pair = jnp.concatenate([low[rows, :], high[rows, :]], axis=0)
            target[rows, :] = mm3(step, split2(pair))

    rough = []
    for q in range(2):
        join_z(moments.at[2 * q], moments.at[2 * q + 1], work_a)
        mix_x(work_a, work_b, lanes, 0, True)
        mix_y(work_b, parents.at[q], lanes, 1, True)
        rough.append(mm3(compress_t, split2(parents[q])).T)
    par[...] = jnp.dot(
        pick_par[...], jnp.concatenate(rough, axis=0), precision=EXACT, preferred_element_type=F32
    )
    join_z(parents.at[0], parents.at[1], work_a)
    mix_x(work_a, work_b, lanes, 2, True)
    mix_y(work_b, work_a, lanes, 3, True)
    rough = mm3(compress_t, split2(work_a[...])).T
    grand[...] = jnp.dot(pick_grand[...], rough, precision=EXACT, preferred_element_type=F32)

    def particle(component, cells, part):
        columns = slice(part * 128, part * 128 + 128)
        if component < 3:
            return pos[component, cells, columns]
        return weighted[cells, columns]

    for buffer, x0, px0, xn in ((xs_low, 0, 0, 0), (xs_high, 6, 2, 7)):
        buffer[0:128, :] = leaf[x0 * 64 : x0 * 64 + 128, :]
        buffer[FACE_PAR : FACE_PAR + 32, :] = par[px0 * 16 : px0 * 16 + 32, :]
        buffer[FACE_GRAND : FACE_GRAND + 8, :] = grand[...]
        for corner, y0, py0, yn in ((FACE, 0, 0, 0), (FACE + CORNER, 6, 2, 7)):
            for i in range(2):
                source = ((x0 + i) * 8 + y0) * 8
                buffer[corner + i * 16 : corner + i * 16 + 16, :] = leaf[source : source + 16, :]
                source = ((px0 + i) * 4 + py0) * 4
                target = corner + COR_PAR + i * 8
                buffer[target : target + 8, :] = par[source : source + 8, :]
            target = corner + COR_GRAND
            buffer[target : target + 8, :] = grand[...]
        for component in range(4):
            for part in range(2):
                row = 2 * component + part
                value = particle(component, slice(xn * 8, xn * 8 + 8), part)
                buffer[pl.ds(FACE_NEAR + row, 8, stride=8), :] = value
                for corner, yn in ((FACE, 0), (FACE + CORNER, 7)):
                    target = corner + COR_NEAR + row
                    buffer[target : target + 1, :] = value[yn : yn + 1, :]
    for buffer, y0, py0, yn in ((ys_low, 0, 0, 0), (ys_high, 6, 2, 7)):
        for x in range(8):
            source = (x * 8 + y0) * 8
            buffer[x * 16 : x * 16 + 16, :] = leaf[source : source + 16, :]
        for x in range(4):
            source = (x * 4 + py0) * 4
            target = FACE_PAR + x * 8
            buffer[target : target + 8, :] = par[source : source + 8, :]
        buffer[FACE_GRAND : FACE_GRAND + 8, :] = grand[...]
        for x in range(8):
            for component in range(4):
                for part in range(2):
                    value = particle(component, slice(x * 8 + yn, x * 8 + yn + 1), part)
                    target = FACE_NEAR + x * 8 + 2 * component + part
                    buffer[target : target + 1, :] = value


def stage_columns(columns, pos, weighted, x_faces, y_faces):
    columns[...] = jnp.zeros_like(columns)
    for component in range(4):
        for part in range(2):
            row = 2 * component + part
            lanes = slice(part * 128, part * 128 + 128)
            own = pos[component, :, lanes] if component < 3 else weighted[:, lanes]
            columns[row, 0:64, :] = own
            for n, buffer in enumerate((*x_faces, *y_faces)):
                columns[row, 64 + 8 * n : 72 + 8 * n, :] = buffer[
                    pl.ds(FACE_NEAR + row, 8, stride=8), :
                ]
            for n, buffer in enumerate(y_faces):
                for side in range(2):
                    source = FACE + side * CORNER + COR_NEAR + row
                    target = 96 + 2 * n + side
                    columns[row, target : target + 1, :] = buffer[source : source + 1, :]


def stage_sources(columns, pick, shifts, sources, squares):
    empty = jnp.zeros((32, 128), F32)
    for component in range(4):
        low = columns[2 * component].T
        high = columns[2 * component + 1].T
        left = jnp.concatenate([empty, low, high[0:32, :]], axis=0)
        right = jnp.concatenate([low[96:128, :], high, empty], axis=0)
        pieces = split3(jnp.concatenate([left, right], axis=1))
        for n, k in enumerate(shifts):
            table = pick[:, k * 128 : k * 128 + 128]
            value = (mm(pieces[0], table) + mm(pieces[1], table)) + mm(pieces[2], table)
            if component == 3:
                sources[3, n] = value
                continue
            offset = (k // 3 - 1, k % 3 - 1, 0)[component] - 0.5
            value = value + offset
            sources[component, n] = -2.0 * value
            if component == 0:
                squares[n] = value * value + SOFTENING
            else:
                squares[n] = squares[n] + value * value


def pair_steps(targets, start, dz, sources, squares, n, base, count, own, sums):
    groups = [
        [targets[component, pl.ds(start + 8 * g, 8), :] for component in range(3)]
        for g in range(4)
    ]
    high = [t[2] - dz for t in groups]
    square = [t[0] * t[0] + t[1] * t[1] + h * h for t, h in zip(groups, high)]
    slot = lax.broadcasted_iota(jnp.int32, (8, 128), 0)
    for s in range(count):
        row = pl.ds(base + s, 1)
        px = jnp.broadcast_to(sources[0, n, row, :], (8, 128))
        py = jnp.broadcast_to(sources[1, n, row, :], (8, 128))
        pz = jnp.broadcast_to(sources[2, n, row, :], (8, 128))
        pw = jnp.broadcast_to(sources[3, n, row, :], (8, 128))
        pq = jnp.broadcast_to(squares[n, row, :], (8, 128))
        for g in range(4):
            distance = (square[g] + pq) + groups[g][0] * px + (groups[g][1] * py + high[g] * pz)
            term = pw * lax.rsqrt(distance)
            if own and s // 8 == g:
                term = jnp.where(slot == s % 8, 0.0, term)
            sums[g] = term if sums[g] is None else sums[g] + term
        yield


def pair_sums(*arguments):
    sums = [None] * 4
    for _ in pair_steps(*arguments, sums):
        pass
    return sums


def near_part(shifts, pos, weighted, x_faces, pick, near, before, columns, sources, squares, targets):
    stage_columns(columns, pos, weighted, x_faces, ())
    stage_sources(columns, pick, shifts, sources, squares)
    for component in range(3):
        targets[component] = lanes_first(pos[component]) - 0.5

    def chunk(c, carry):
        start = pl.multiple_of(c * 32, 32)
        for g in range(4):
            rows = pl.ds(start + 8 * g, 8)
            near[rows, :] = jnp.zeros((8, 128), F32) if before is None else before[rows, :]
        for dz in (-1, 0, 1):
            for n, k in enumerate(shifts):
                sums = pair_sums(
                    targets, start, float(dz), sources, squares, n,
                    pl.multiple_of(start + 32 * (1 + dz), 32), 32, k == 4 and dz == 0,
                )
                for g in range(4):
                    rows = pl.ds(start + 8 * g, 8)
                    near[rows, :] = near[rows, :] + sums[g]
        return carry

    lax.fori_loop(0, 4, chunk, 0)


def near_own_kernel(pos, weighted, pick, near, columns, sources, squares, targets):
    near_part((4,), pos, weighted, (), pick, near, None, columns, sources, squares, targets)


def near_x_kernel(
    pos, weighted, x_low, x_high, pick, before, near, columns, sources, squares, targets
):
    near_part(
        (1, 7), pos, weighted, (x_low, x_high), pick, near, before,
        columns, sources, squares, targets,
    )


SIDEWAYS = (0, 2, 3, 5, 6, 8)


ROW_STARTS = (0, 49, 98, 138, 178, 218, 267, 316)


def downward_kernel(
    pos, weighted, counts, before, leaf, par, grand, x_low, x_high, y_low, y_high, operators,
    expand, lanes, down_z, spread, near_pick, leaf_pick, small_pick, place_leaf, place_small,
    out,
    weights, staged, small, leaf_high, leaf_low, small_high, small_low, right_high, right_low,
    sums, flat, basis_x, basis_y, basis_z, local, work_a, work_b, work_c, far,
    near, columns, sources, squares, targets, arrivals,
):
    copies = [
        pltpu.make_async_copy(
            operators.at[pl.ds(ROW_STARTS[n], ROW_STARTS[n + 1] - ROW_STARTS[n])],
            weights.at[pl.ds(ROW_STARTS[n], ROW_STARTS[n + 1] - ROW_STARTS[n])],
            arrivals.at[n],
        )
        for n in range(7)
    ]
    for copy in copies:
        copy.start()

    near[...] = before[...]
    stage_columns(columns, pos, weighted, (x_low, x_high), (y_low, y_high))
    stage_sources(columns, near_pick, SIDEWAYS, sources, squares)
    for component in range(3):
        flat[component] = lanes_first(pos[component])
        targets[component] = flat[component] - 0.5

    def unit_steps(unit, chunks, results):
        level = unit // 12
        dz = (level - 1).astype(F32) if isinstance(level, jax.Array) else float(level - 1)
        for c in chunks:
            base = pl.multiple_of(32 * c + 32 * level + 16 * (unit % 2), 16)
            results[c] = [None] * 4
            yield from pair_steps(
                targets, 32 * c, dz, sources, squares, unit % 12 // 2, base, 16, False, results[c]
            )

    staged[...] = jnp.zeros_like(staged)
    small[...] = jnp.zeros_like(small)
    faces = (x_low, x_high, y_low, y_high)
    for z in range(8):
        columns = slice(z * 128, z * 128 + 128)
        staged[0:64, columns] = leaf[pl.ds(z, 64, stride=8), :]
        for n, buffer in enumerate(faces):
            target = 64 + 16 * n
            staged[target : target + 16, columns] = buffer[pl.ds(z, 16, stride=8), :]
        for n, buffer in enumerate((y_low, y_high)):
            for side in range(2):
                target = 128 + 16 * n + 8 * side
                source = FACE + side * CORNER + z
                staged[target : target + 4, columns] = buffer[pl.ds(source, 4, stride=8), :]
    for z in range(4):
        columns = slice(z % 2 * 128, z % 2 * 128 + 128)
        top = z // 2 * 64
        small[top : top + 16, columns] = par[pl.ds(z, 16, stride=4), :]
        for n, buffer in enumerate(faces):
            target = top + 16 + 8 * n
            small[target : target + 8, columns] = buffer[pl.ds(FACE_PAR + z, 8, stride=4), :]
        for n, buffer in enumerate((y_low, y_high)):
            for side in range(2):
                target = top + 48 + 8 * n + 4 * side
                source = FACE + side * CORNER + COR_PAR + z
                small[target : target + 4, columns] = buffer[pl.ds(source, 4, stride=4), :]
    for z in range(2):
        columns = slice(z * 128, z * 128 + 128)
        small[128:132, columns] = grand[pl.ds(z, 4, stride=2), :]
        for n, buffer in enumerate(faces):
            target = 132 + 4 * n
            small[target : target + 4, columns] = buffer[pl.ds(FACE_GRAND + z, 4, stride=2), :]
        for n, buffer in enumerate((y_low, y_high)):
            for side in range(2):
                target = 148 + 8 * n + 4 * side
                source = FACE + side * CORNER + COR_GRAND + z
                small[target : target + 4, columns] = buffer[pl.ds(source, 4, stride=2), :]

    blank = jnp.zeros((36, 16, 256), BF16)
    for target in (leaf_high, leaf_low):
        target[:, 0] = blank
        target[:, 5] = blank
    for zp in range(4):
        pieces = split2(staged[:, zp * 256 : zp * 256 + 256])
        for piece, target in zip(pieces, (leaf_high, leaf_low)):
            target[:, zp + 1] = mm(leaf_pick[...], piece).astype(BF16).reshape(36, 16, 256)
    for piece, target in zip(split2(small[...]), (small_high, small_low)):
        target[...] = mm(small_pick[...], piece).astype(BF16).reshape(36, 3, 16, 256)

    sums[...] = jnp.zeros_like(sums)

    def left(high, v, d):
        main, rest = (leaf_high, small_high) if high else (leaf_low, small_low)
        return jnp.concatenate(
            [main[v, pl.ds(d, 4)].reshape(64, 256), rest[v, d]], axis=0
        )

    def translate(dx, dy, xs, ys, base, beside, unit, chunks):
        split = {}
        for n, dz in enumerate((-3, -2, 2, 3) if beside else range(-3, 4)):
            split[dz] = split2(weights[base + n])
        none = jnp.zeros((128, 128), BF16)
        right = {}
        for d in range(3):
            for which in range(2):
                right[d, which] = jnp.concatenate(
                    [
                        jnp.concatenate(
                            [
                                split[2 * (d - 1) + source - side][which]
                                if 2 * (d - 1) + source - side in split
                                else none
                                for side in range(2)
                            ],
                            axis=1,
                        )
                        for source in range(2)
                    ],
                    axis=0,
                )
        pass
        sides = [(px, py) for px in xs for py in ys]
        variants = [(px + dx + 2) * 6 + (py + dy + 2) for px, py in sides]
        jobs = []
        for d in (0, 2) if beside else (0, 1, 2):
            upper = jnp.concatenate([left(True, v, d) for v in variants], axis=0)
            lower = jnp.concatenate([left(False, v, d) for v in variants], axis=0)
            jobs += [(jnp.concatenate([upper, lower], axis=0), right[d, 0]), (upper, right[d, 1])]
        results = {}
        steps = unit_steps(unit, chunks, results)
        todo = 16 * len(chunks)
        done = 0
        total = None
        size = 80 * len(sides)
        for n, (a, b) in enumerate(jobs):
            term = mm(a, b)
            if a.shape[0] > size:
                term = term[:size] + term[size:]
            total = term if total is None else total + term
            while done < todo * (n + 1) // len(jobs):
                next(steps)
                done += 1
        for n, (px, py) in enumerate(sides):
            sums[px * 2 + py] = sums[px * 2 + py] + total[n * 80 : n * 80 + 80, :]
        for c in chunks:
            for g in range(4):
                rows = slice(32 * c + 8 * g, 32 * c + 8 * g + 8)
                near[rows, :] = near[rows, :] + results[c][g]

    both = (0, 1)
    every = (0, 1, 2, 3)
    unit = 0
    for n, dx in enumerate(range(-3, 4)):
        copies[n].wait()
        start = ROW_STARTS[n]
        xs = (1,) if dx == -3 else (0,) if dx == 3 else both
        middle = abs(dx) <= 1
        outer = abs(dx) == 3
        low, high = ((0,), (1,)) if dx == -3 else ((2,), (3,)) if dx == 3 else ((0, 1), (2, 3))
        row = 35 if outer else 30 + dx + 2
        translate(dx, -3, xs, (1,), start, False, row, low)
        if middle:
            translate(dx, -2, xs, both, start + 7, False, unit, every)

            def step(i, carry, dx=dx, xs=xs, start=start):
                place = 16 + 3 * (dx + 1) + i
                translate(dx, i - 1, xs, both, start + 14 + 4 * i, True, place, every)
                return carry

            lax.fori_loop(0, 3, step, 0)
            translate(dx, 2, xs, both, start + 26, False, unit + 1, every)
            unit += 2
            last = start + 33
        else:
            chunks = ((0, 1) if dx < 0 else (2, 3)) if outer else every

            def step(i, carry, dx=dx, xs=xs, start=start, unit=unit, chunks=chunks, outer=outer):
                place = 25 + i if outer else unit + i
                translate(dx, i - 2, xs, both, start + 7 + 7 * i, False, place, chunks)
                return carry

            lax.fori_loop(0, 5, step, 0)
            unit += 0 if outer else 5
            last = start + 42
        translate(dx, 3, xs, (0,), last, False, row, high)

    grow = split2(expand[...].T)
    pairs = [(px, py) for px in both for py in both]

    def expanded(rows, place):
        flipped = split2(rows.T)
        placed = tuple(mm(piece, place).astype(BF16) for piece in flipped)
        return mm3(grow, placed)

    pieces = []
    for q in range(2):
        for z in range(2):
            for px, py in pairs:
                rows = slice(64 + 4 * z, 68 + 4 * z)
                pieces.append(sums[px * 2 + py, rows, q * 128 : q * 128 + 128] * 0.5)
    for px, py in pairs:
        for z in range(2):
            pieces.append(sums[px * 2 + py, 72:73, z * 128 : z * 128 + 128] * 0.25)
    pieces.append(jnp.zeros((56, 128), F32))
    coarse = jnp.concatenate(pieces, axis=0)
    step = split2(down_z[...])

    work_a[...] = expanded(coarse, place_small[2])
    mix_x(work_a, work_b, lanes, 2, False)
    mix_y(work_b, work_c, lanes, 3, False)

    for q in range(2):
        side = tuple(piece[q * 128 : q * 128 + 128, :] for piece in step)
        work_a[...] = expanded(coarse, place_small[q])
        for block in range(4):
            rows = slice(block * 128, block * 128 + 128)
            work_a[rows, :] = work_a[rows, :] + mm3(side, split2(work_c[rows, :]))
        mix_x(work_a, work_b, lanes, 0, False)
        mix_y(work_b, work_a, lanes, 1, False)
        for cz in range(2):
            rows = [
                sums[px * 2 + py, (q + 2 * z) * 16 : (q + 2 * z) * 16 + 16, cz * 128 : cz * 128 + 128]
                for z in range(2)
                for px, py in pairs
            ]
            side = tuple(piece[cz * 128 : cz * 128 + 128, :] for piece in step)
            local[2 * q + cz] = expanded(jnp.concatenate(rows, axis=0), place_leaf[...])
            for block in range(4):
                part = slice(block * 128, block * 128 + 128)
                local[2 * q + cz, part, :] = local[2 * q + cz, part, :] + mm3(
                    side, split2(work_a[part, :])
                )

    def chunk(c, carry):
        start = pl.multiple_of(c * 32, 32)
        rows = pl.ds(start, 32)
        for a, value in enumerate(basis(flat[0, rows, :])):
            basis_x[a * 32 : a * 32 + 32, :] = value
        for a, value in enumerate(basis(flat[1, rows, :])):
            basis_y[a * 32 : a * 32 + 32, :] = value
        for a, value in enumerate(basis(flat[2, rows, :])):
            basis_z[pl.ds(a, 32, stride=8), :] = value

        def slots(n, carry):
            first = 2 * n
            totals = [None, None]
            along_y = [[bcast(basis_y, b * 32 + first + j) for b in range(8)] for j in range(2)]
            for a in range(8):
                inner = [None, None]
                for b in range(8):
                    value = local[c, (a * 8 + b) * 8 : (a * 8 + b) * 8 + 8, :]
                    for j in range(2):
                        term = value * along_y[j][b]
                        inner[j] = term if inner[j] is None else inner[j] + term
                for j in range(2):
                    term = inner[j] * bcast(basis_x, a * 32 + first + j)
                    totals[j] = term if totals[j] is None else totals[j] + term
            for j in range(2):
                along_z = basis_z[pl.ds(pl.multiple_of((first + j) * 8, 8), 8), :]
                far[pl.ds(start + first + j, 1), :] = jnp.sum(
                    totals[j] * along_z, axis=0, keepdims=True
                )
            return carry

        lax.fori_loop(0, 16, slots, 0, unroll=2)
        return carry

    lax.fori_loop(0, 4, chunk, 0)
    total = (far[...] + near[...]).T
    occupied = occupied_slots(counts, spread)
    out[...] = jnp.concatenate([total[0:64, :], total[64:128, :]], axis=1) * occupied


def vmem(count):
    return [pl.BlockSpec(memory_space=pltpu.VMEM) for _ in range(count)]


def shaped(*dims):
    return jax.ShapeDtypeStruct(dims, F32)


def neighbours(low, high, axis):
    count = lax.axis_size(axis)
    up = [(i, i + 1) for i in range(count - 1)]
    down = [(target, source) for source, target in up]
    return lax.ppermute(high, axis, up), lax.ppermute(low, axis, down)


def per_device(positions, charges, counts, compress, operators, expand):
    const = {name: jnp.asarray(value) for name, value in make_constants().items()}
    pos = positions.reshape(3, 64, 256)
    cells = counts.reshape(64, 8)
    limit = pltpu.CompilerParams(vmem_limit_bytes=56 * 1024 * 1024)
    leaf, par, grand, xs_low, xs_high, ys_low, ys_high, weighted = pl.pallas_call(
        upward_kernel,
        out_shape=[
            shaped(512, 128), shaped(64, 128), shaped(8, 128),
            shaped(PACKED, 128), shaped(PACKED, 128), shaped(FACE, 128), shaped(FACE, 128),
            shaped(64, 256),
        ],
        in_specs=vmem(9),
        out_specs=vmem(8),
        scratch_shapes=[
            pltpu.VMEM((4, 128, 128), F32),
            pltpu.VMEM((256, 128), F32),
            pltpu.VMEM((256, 128), F32),
            pltpu.VMEM((256, 128), F32),
            pltpu.VMEM((4, 512, 128), F32),
            pltpu.VMEM((512, 128), F32),
            pltpu.VMEM((512, 128), F32),
            pltpu.VMEM((2, 512, 128), F32),
        ],
        compiler_params=limit,
        name="upward",
    )(
        pos, charges.reshape(64, 256), cells, compress, const["lanes"], const["up_z"],
        const["pick_par"], const["pick_grand"], const["spread"],
    )
    x_low, x_high = neighbours(xs_low, xs_high, "gx")
    def near_scratch(count):
        return [
            pltpu.VMEM((8, 128, 128), F32),
            pltpu.VMEM((4, count, 192, 128), F32),
            pltpu.VMEM((count, 192, 128), F32),
            pltpu.VMEM((3, 128, 128), F32),
        ]

    near_own = pl.pallas_call(
        near_own_kernel,
        out_shape=shaped(128, 128),
        in_specs=vmem(3),
        out_specs=vmem(1)[0],
        scratch_shapes=near_scratch(1),
        compiler_params=limit,
        cost_estimate=pl.CostEstimate(flops=10**7, bytes_accessed=10**7, transcendentals=0),
        name="near_own",
    )(pos, weighted, const["near_pick"])
    near_own, x_low, x_high = lax.optimization_barrier((near_own, x_low, x_high))
    first, second = slice(FACE, FACE + CORNER), slice(FACE + CORNER, PACKED)
    y_low, y_high = neighbours(
        jnp.concatenate([ys_low, x_low[first], x_high[first]], axis=0),
        jnp.concatenate([ys_high, x_low[second], x_high[second]], axis=0),
        "gy",
    )
    near = pl.pallas_call(
        near_x_kernel,
        out_shape=shaped(128, 128),
        in_specs=vmem(6),
        out_specs=vmem(1)[0],
        scratch_shapes=near_scratch(2),
        compiler_params=limit,
        cost_estimate=pl.CostEstimate(flops=2 * 10**7, bytes_accessed=2 * 10**7, transcendentals=0),
        name="near_x",
    )(pos, weighted, x_low, x_high, const["near_pick"], near_own)
    result = pl.pallas_call(
        downward_kernel,
        out_shape=shaped(64, 256),
        in_specs=vmem(11) + [pl.BlockSpec(memory_space=pl.ANY)] + vmem(9),
        out_specs=vmem(1)[0],
        scratch_shapes=[
            pltpu.VMEM((316, 128, 128), F32),
            pltpu.VMEM((256, 1024), F32),
            pltpu.VMEM((256, 256), F32),
            pltpu.VMEM((36, 6, 16, 256), BF16),
            pltpu.VMEM((36, 6, 16, 256), BF16),
            pltpu.VMEM((36, 3, 16, 256), BF16),
            pltpu.VMEM((36, 3, 16, 256), BF16),
            pltpu.VMEM((3, 256, 256), BF16),
            pltpu.VMEM((3, 256, 256), BF16),
            pltpu.VMEM((4, 80, 256), F32),
            pltpu.VMEM((3, 128, 128), F32),
            pltpu.VMEM((256, 128), F32),
            pltpu.VMEM((256, 128), F32),
            pltpu.VMEM((256, 128), F32),
            pltpu.VMEM((4, 512, 128), F32),
            pltpu.VMEM((512, 128), F32),
            pltpu.VMEM((512, 128), F32),
            pltpu.VMEM((512, 128), F32),
            pltpu.VMEM((128, 128), F32),
            pltpu.VMEM((128, 128), F32),
            *near_scratch(6),
            pltpu.SemaphoreType.DMA((7,)),
        ],
        compiler_params=limit,
        name="downward",
    )(
        pos, weighted, cells, near, leaf, par, grand, x_low, x_high, y_low, y_high, operators, expand,
        const["lanes"], const["down_z"], const["spread"], const["near_pick"], const["leaf_pick"],
        const["small_pick"], const["place_leaf"], const["place_small"],
    )
    return result.reshape(8, 8, 256)


def solution(mesh):
    placed = (P(None, "gx", "gy", None), P("gx", "gy", None), P("gx", "gy", None), P(), P(), P())
    return jax.shard_map(
        per_device, mesh=mesh, in_specs=placed, out_specs=P("gx", "gy", None), check_vma=False
    )
```

```python
import math

import jax
import jax.numpy as jnp
import numpy as np
from jax import lax
from jax.experimental import pallas as pl
from jax.experimental.pallas import tpu as pltpu
from jax.sharding import PartitionSpec as P

F32 = jnp.float32
BF16 = jnp.bfloat16
SOFTENING = 0.01
EXACT = lax.Precision.HIGHEST

FACE = 232
CORNER = 64
PACKED = FACE + 2 * CORNER
FACE_PAR, FACE_GRAND, FACE_NEAR = 128, 160, 168
COR_PAR, COR_GRAND, COR_NEAR = 32, 48, 56


SIDEWAYS = (0, 2, 3, 5, 6, 8)


def node_cos():
    return np.array(
        [[math.cos(math.pi * k * (2 * a + 1) / 16) for a in range(8)] for k in range(8)]
    )


def cheb_numpy(points):
    series = np.cos(np.arange(1, 8)[:, None] * np.arccos(points)[None, :])
    return 1 / 8 + 2 / 8 * node_cos()[1:].T @ series


def transfer_factor():
    nodes = np.cos(np.pi * (2 * np.arange(8) + 1) / 16)
    points = 0.5 * (nodes[None, :] + np.array([-1.0, 1.0])[:, None])
    weights = cheb_numpy(points.reshape(-1)).reshape(8, 2, 8)
    return weights.transpose(1, 2, 0)


def make_constants():
    factor = transfer_factor()
    lane = np.arange(128)
    lane_z, lane_x, lane_y = lane // 64, lane // 8 % 8, lane % 8
    lanes = np.zeros((4, 64, 128))
    for level in range(2):
        for which, coordinate in ((0, lane_x), (1, lane_y)):
            side = coordinate >> level & 1
            lanes[2 * level + which] = factor[side].transpose(1, 2, 0).reshape(64, 128)
    up_z = np.zeros((16, 8, 2, 16, 8))
    for block in range(16):
        for side in range(2):
            up_z[block, :, side, block, :] = factor[side].T
    up_z = up_z.reshape(128, 256)
    pick_par = np.zeros((64, 256))
    for x in range(4):
        for y in range(4):
            for z in range(4):
                pick_par[(x * 4 + y) * 4 + z, z % 2 * 128 + z // 2 * 64 + 2 * x * 8 + 2 * y] = 1
    pick_grand = np.zeros((8, 128))
    for x in range(2):
        for y in range(2):
            for z in range(2):
                pick_grand[(x * 2 + y) * 2 + z, z * 64 + 4 * x * 8 + 4 * y] = 1
    spread = np.kron(np.eye(8), np.ones((1, 32)))

    near_row = {}
    for x in range(8):
        for y in range(8):
            near_row[x, y] = x * 8 + y
    for y in range(8):
        near_row[-1, y] = 64 + y
        near_row[8, y] = 72 + y
        near_row[y, -1] = 80 + y
        near_row[y, 8] = 88 + y
    near_row[-1, -1], near_row[8, -1], near_row[-1, 8], near_row[8, 8] = 96, 97, 98, 99
    near_pick = np.zeros((256, 9, 128))
    for k in range(9):
        dx, dy = k // 3 - 1, k % 3 - 1
        for ln in range(128):
            row = near_row[int(lane_x[ln]) + dx, int(lane_y[ln]) + dy]
            near_pick[lane_z[ln] * 128 + row, k, ln] = 1
    near_pick = near_pick[:, SIDEWAYS + (1, 7, 4)].reshape(256, 1152)

    leaf_row = {}
    for x in range(8):
        for y in range(8):
            leaf_row[x, y] = x * 8 + y
    for i in range(2):
        for y in range(8):
            leaf_row[i - 2, y] = 64 + i * 8 + y
            leaf_row[8 + i, y] = 80 + i * 8 + y
            leaf_row[y, i - 2] = 96 + y * 2 + i
            leaf_row[y, 8 + i] = 112 + y * 2 + i
        for j in range(2):
            leaf_row[i - 2, j - 2] = 128 + i * 2 + j
            leaf_row[8 + i, j - 2] = 136 + i * 2 + j
            leaf_row[i - 2, 8 + j] = 144 + i * 2 + j
            leaf_row[8 + i, 8 + j] = 152 + i * 2 + j
    leaf_pick = np.zeros((36, 16, 256))
    for v in range(36):
        sx, sy = v // 6 - 2, v % 6 - 2
        for r in range(16):
            leaf_pick[v, r, leaf_row[2 * (r // 4) + sx, 2 * (r % 4) + sy]] = 1
    leaf_pick = leaf_pick.reshape(576, 256)

    par_row = {}
    for x in range(4):
        for y in range(4):
            par_row[x, y] = x * 4 + y
    for i in range(2):
        for y in range(4):
            par_row[i - 2, y] = 16 + i * 4 + y
            par_row[4 + i, y] = 24 + i * 4 + y
            par_row[y, i - 2] = 32 + y * 2 + i
            par_row[y, 4 + i] = 40 + y * 2 + i
        for j in range(2):
            par_row[i - 2, j - 2] = 48 + i * 2 + j
            par_row[4 + i, j - 2] = 52 + i * 2 + j
            par_row[i - 2, 4 + j] = 56 + i * 2 + j
            par_row[4 + i, 4 + j] = 60 + i * 2 + j
    grand_row = {}
    order = [(0, 0), (-2, 0), (2, 0), (0, -2), (0, 2), (-2, -2), (2, -2), (-2, 2), (2, 2)]
    for n, (ox, oy) in enumerate(order):
        for i in range(2):
            for j in range(2):
                grand_row[ox + i, oy + j] = 128 + n * 4 + i * 2 + j
    small_pick = np.zeros((36, 3, 16, 256))
    for v in range(36):
        sx, sy = v // 6 - 2, v % 6 - 2
        for d in range(3):
            for r in range(8):
                zp = r // 4 + d - 1
                if 0 <= zp < 2:
                    row = par_row[2 * (r // 2 % 2) + sx, 2 * (r % 2) + sy]
                    small_pick[v, d, r, zp * 64 + row] = 1
            if d == 1:
                small_pick[v, d, 8, grand_row[sx, sy]] = 1
    small_pick = small_pick.reshape(1728, 256)

    place_leaf = np.zeros((128, 128))
    for z in range(2):
        for px in range(2):
            for py in range(2):
                for xp in range(4):
                    for yp in range(4):
                        row = ((z * 2 + px) * 2 + py) * 16 + xp * 4 + yp
                        place_leaf[row, z * 64 + (2 * xp + px) * 8 + 2 * yp + py] = 1
    place_small = np.zeros((3, 128, 128))
    for ln in range(128):
        z, x, y = int(lane_z[ln]), int(lane_x[ln]) >> 1, int(lane_y[ln]) >> 1
        for q in range(2):
            row = (((q * 2 + z) * 2 + x % 2) * 2 + y % 2) * 4 + x // 2 * 2 + y // 2
            place_small[q, row, ln] = 1
        place_small[2, 64 + ((x >> 1) * 2 + (y >> 1)) * 2 + z, ln] = 1

    def half(array):
        return np.asarray(array, np.float32).astype(jnp.bfloat16)

    return dict(
        lanes=np.asarray(lanes, np.float32),
        up_z=np.asarray(up_z, np.float32),
        down_z=np.asarray(up_z.T, np.float32),
        pick_par=np.asarray(pick_par, np.float32),
        pick_grand=np.asarray(pick_grand, np.float32),
        spread=half(spread),
        near_pick=half(near_pick),
        leaf_pick=half(leaf_pick),
        small_pick=half(small_pick),
        place_leaf=half(place_leaf),
        place_small=half(place_small),
    )


def mm(a, b):
    return jnp.dot(a, b, preferred_element_type=F32)


def split2(x):
    high = x.astype(BF16)
    return high, (x - high.astype(F32)).astype(BF16)


def split3(x):
    high = x.astype(BF16)
    rest = x - high.astype(F32)
    mid = rest.astype(BF16)
    return high, mid, (rest - mid.astype(F32)).astype(BF16)


def mm3(a, b):
    a_high, a_low = a
    b_high, b_low = b
    return mm(a_high, b_high) + (mm(a_high, b_low) + mm(a_low, b_high))


def lanes_first(block):
    return jnp.concatenate([block[:, :128], block[:, 128:]], axis=0).T


def basis(points):
    u = jnp.clip(2.0 * points - 1.0, -1.0, 1.0)
    series = [None, u]
    for _ in range(2, 8):
        before = series[-2] if len(series) > 2 else 1.0
        series.append(2.0 * u * series[-1] - before)
    table = node_cos()
    weights = [None] * 8
    for a in range(4):
        even = 0.125
        odd = None
        for k in range(1, 8):
            term = series[k] * np.float32(0.25 * table[k, a])
            if k % 2 == 0:
                even = even + term
            else:
                odd = term if odd is None else odd + term
        weights[a] = even + odd
        weights[7 - a] = even - odd
    return weights


def occupied_slots(counts_ref, spread_ref):
    limits = mm(counts_ref[...].astype(F32).astype(BF16), spread_ref[...])
    slot = lax.broadcasted_iota(jnp.int32, (64, 256), 1) & 31
    return jnp.where(slot.astype(F32) < limits, 1.0, 0.0)


def bcast(ref, row):
    return jnp.broadcast_to(ref[pl.ds(row, 1), :], (8, 128))


def mix_x(source, target, lanes_ref, which, up):
    for out in range(8):
        total = None
        for inner in range(8):
            row = inner * 8 + out if up else out * 8 + inner
            term = lanes_ref[which, row : row + 1, :] * source[inner * 64 : inner * 64 + 64, :]
            total = term if total is None else total + term
        if up:
            shift = 8 << (which // 2)
            total = total + pltpu.roll(total, 128 - shift, 1)
        target[out * 64 : out * 64 + 64, :] = total


def mix_y(source, target, lanes_ref, which, up):
    def one(a, carry):
        start = pl.multiple_of(a * 64, 64)
        rows = [source[pl.ds(start + 8 * b, 8), :] for b in range(8)]
        for out in range(8):
            total = None
            for inner in range(8):
                row = inner * 8 + out if up else out * 8 + inner
                term = lanes_ref[which, row : row + 1, :] * rows[inner]
                total = term if total is None else total + term
            if up:
                shift = 1 << (which // 2)
                total = total + pltpu.roll(total, 128 - shift, 1)
            target[pl.ds(start + 8 * out, 8), :] = total
        return carry

    lax.fori_loop(0, 8, one, 0)


def upward_kernel(
    pos, charges, counts, compress, lanes, up_z, pick_par, pick_grand, spread,
    leaf, par, grand, xs_low, xs_high, ys_low, ys_high, weighted,
    flat, basis_x, basis_y, basis_z, moments, work_a, work_b, parents,
):
    w = charges[...] * occupied_slots(counts, spread)
    weighted[...] = w
    for component in range(3):
        flat[component] = lanes_first(pos[component])
    flat[3] = lanes_first(w)

    def chunk(c, carry):
        rows = pl.ds(pl.multiple_of(c * 32, 32), 32)
        mass = flat[3, rows, :]
        for a, value in enumerate(basis(flat[0, rows, :])):
            basis_x[a * 32 : a * 32 + 32, :] = value
        for a, value in enumerate(basis(flat[1, rows, :])):
            basis_y[a * 32 : a * 32 + 32, :] = value * mass
        for a, value in enumerate(basis(flat[2, rows, :])):
            basis_z[pl.ds(a, 32, stride=8), :] = value
        for half in range(2):

            def slot(s, sums):
                along_z = basis_z[pl.ds(pl.multiple_of(s * 8, 8), 8), :]
                along_y = [bcast(basis_y, b * 32 + s) for b in range(8)]
                result = []
                for a in range(4):
                    part = bcast(basis_x, (half * 4 + a) * 32 + s) * along_z
                    for b in range(8):
                        result.append(sums[a * 8 + b] + part * along_y[b])
                return tuple(result)

            zero = jnp.zeros((8, 128), F32)
            sums = lax.fori_loop(0, 32, slot, (zero,) * 32, unroll=8)
            for n in range(32):
                moments[c, (half * 32 + n) * 8 : (half * 32 + n) * 8 + 8, :] = sums[n]
        return carry

    lax.fori_loop(0, 4, chunk, 0)
    compress_t = split2(compress[...].T)
    for first in (0, 2):
        pair = jnp.concatenate([moments[first], moments[first + 1]], axis=1)
        small = mm3(compress_t, split2(pair)).T
        for c in (first, first + 1):
            for z in range(2):
                top = (c - first) * 128 + z * 64
                leaf[pl.ds(c + 4 * z, 64, stride=8), :] = small[top : top + 64, :]

    step = split2(up_z[...])
    for block in range(4):
        rows = slice(block * 128, block * 128 + 128)
        pair = jnp.concatenate(
            [
                jnp.concatenate([moments[cz, rows, :], moments[2 + cz, rows, :]], axis=1)
                for cz in range(2)
            ],
            axis=0,
        )
        joined = mm3(step, split2(pair))
        for q in range(2):
            parents[q, rows, :] = joined[:, 128 * q : 128 * q + 128]
    for q in range(2):
        mix_x(parents.at[q], work_b, lanes, 0, True)
        mix_y(work_b, parents.at[q], lanes, 1, True)
    rough = mm3(compress_t, split2(jnp.concatenate([parents[0], parents[1]], axis=1))).T
    par[...] = jnp.dot(pick_par[...], rough, precision=EXACT, preferred_element_type=F32)
    for block in range(4):
        rows = slice(block * 128, block * 128 + 128)
        pair = jnp.concatenate([parents[0, rows, :], parents[1, rows, :]], axis=0)
        work_a[rows, :] = mm3(step, split2(pair))
    mix_x(work_a, work_b, lanes, 2, True)
    mix_y(work_b, work_a, lanes, 3, True)
    rough = mm3(compress_t, split2(work_a[...])).T
    grand[...] = jnp.dot(pick_grand[...], rough, precision=EXACT, preferred_element_type=F32)

    def particle(component, cells, part):
        columns = slice(part * 128, part * 128 + 128)
        if component < 3:
            return pos[component, cells, columns]
        return weighted[cells, columns]

    for buffer, x0, px0, xn in ((xs_low, 0, 0, 0), (xs_high, 6, 2, 7)):
        buffer[0:128, :] = leaf[x0 * 64 : x0 * 64 + 128, :]
        buffer[FACE_PAR : FACE_PAR + 32, :] = par[px0 * 16 : px0 * 16 + 32, :]
        buffer[FACE_GRAND : FACE_GRAND + 8, :] = grand[...]
        for corner, y0, py0, yn in ((FACE, 0, 0, 0), (FACE + CORNER, 6, 2, 7)):
            for i in range(2):
                source = ((x0 + i) * 8 + y0) * 8
                buffer[corner + i * 16 : corner + i * 16 + 16, :] = leaf[source : source + 16, :]
                source = ((px0 + i) * 4 + py0) * 4
                target = corner + COR_PAR + i * 8
                buffer[target : target + 8, :] = par[source : source + 8, :]
            target = corner + COR_GRAND
            buffer[target : target + 8, :] = grand[...]
        for component in range(4):
            for part in range(2):
                row = 2 * component + part
                value = particle(component, slice(xn * 8, xn * 8 + 8), part)
                buffer[pl.ds(FACE_NEAR + row, 8, stride=8), :] = value
                for corner, yn in ((FACE, 0), (FACE + CORNER, 7)):
                    target = corner + COR_NEAR + row
                    buffer[target : target + 1, :] = value[yn : yn + 1, :]
    for buffer, y0, py0, yn in ((ys_low, 0, 0, 0), (ys_high, 6, 2, 7)):
        for x in range(8):
            source = (x * 8 + y0) * 8
            buffer[x * 16 : x * 16 + 16, :] = leaf[source : source + 16, :]
        for x in range(4):
            source = (x * 4 + py0) * 4
            target = FACE_PAR + x * 8
            buffer[target : target + 8, :] = par[source : source + 8, :]
        buffer[FACE_GRAND : FACE_GRAND + 8, :] = grand[...]
        for x in range(8):
            for component in range(4):
                for part in range(2):
                    value = particle(component, slice(x * 8 + yn, x * 8 + yn + 1), part)
                    target = FACE_NEAR + x * 8 + 2 * component + part
                    buffer[target : target + 1, :] = value


def stage_columns(columns, pos, weighted, x_faces, y_faces):
    columns[...] = jnp.zeros_like(columns)
    for component in range(4):
        for part in range(2):
            row = 2 * component + part
            lanes = slice(part * 128, part * 128 + 128)
            own = pos[component, :, lanes] if component < 3 else weighted[:, lanes]
            columns[row, 0:64, :] = own
            for n, buffer in enumerate((*x_faces, *y_faces)):
                columns[row, 64 + 8 * n : 72 + 8 * n, :] = buffer[
                    pl.ds(FACE_NEAR + row, 8, stride=8), :
                ]
            for n, buffer in enumerate(y_faces):
                for side in range(2):
                    source = FACE + side * CORNER + COR_NEAR + row
                    target = 96 + 2 * n + side
                    columns[row, target : target + 1, :] = buffer[source : source + 1, :]


def stage_sources(columns, pick, column, shifts, sources, squares):
    empty = jnp.zeros((32, 128), F32)
    for component in range(4):
        low = columns[2 * component].T
        high = columns[2 * component + 1].T
        left = jnp.concatenate([empty, low, high[0:32, :]], axis=0)
        right = jnp.concatenate([low[96:128, :], high, empty], axis=0)
        pieces = jnp.concatenate(split3(jnp.concatenate([left, right], axis=1)), axis=0)
        for first in range(0, len(shifts), 2):
            width = 128 * min(2, len(shifts) - first)
            chosen = mm(pieces, pick[:, column + 128 * first : column + 128 * first + width])
            chosen = (chosen[0:192] + chosen[192:384]) + chosen[384:576]
            for n in range(first, first + width // 128):
                value = chosen[:, 128 * (n - first) : 128 * (n - first) + 128]
                if component == 3:
                    sources[3, n] = value
                    continue
                offset = (shifts[n] // 3 - 1, shifts[n] % 3 - 1, 0)[component] - 0.5
                value = value + offset
                sources[component, n] = -2.0 * value
                if component == 0:
                    squares[n] = value * value + SOFTENING
                else:
                    squares[n] = squares[n] + value * value


def pair_steps(targets, start, dz, sources, squares, n, base, count, own, sums):
    groups = [
        [targets[component, pl.ds(start + 8 * g, 8), :] for component in range(3)]
        for g in range(4)
    ]
    high = [t[2] - dz for t in groups]
    square = [t[0] * t[0] + t[1] * t[1] + h * h for t, h in zip(groups, high)]
    slot = lax.broadcasted_iota(jnp.int32, (8, 128), 0)
    for s in range(count):
        row = pl.ds(base + s, 1)
        px = jnp.broadcast_to(sources[0, n, row, :], (8, 128))
        py = jnp.broadcast_to(sources[1, n, row, :], (8, 128))
        pz = jnp.broadcast_to(sources[2, n, row, :], (8, 128))
        pw = jnp.broadcast_to(sources[3, n, row, :], (8, 128))
        pq = jnp.broadcast_to(squares[n, row, :], (8, 128))
        for g in range(4):
            distance = (square[g] + pq) + groups[g][0] * px + (groups[g][1] * py + high[g] * pz)
            term = pw * lax.rsqrt(distance)
            if own and s // 8 == g:
                term = jnp.where(slot == s % 8, 0.0, term)
            sums[g] = term if sums[g] is None else sums[g] + term
        yield


def pair_sums(*arguments):
    sums = [None] * 4
    for _ in pair_steps(*arguments, sums):
        pass
    return sums


def near_part(shifts, pos, weighted, x_faces, pick, near, before, columns, sources, squares, targets):
    stage_columns(columns, pos, weighted, x_faces, ())
    stage_sources(columns, pick, 1024 if shifts == (4,) else 768, shifts, sources, squares)
    for component in range(3):
        targets[component] = lanes_first(pos[component]) - 0.5

    def chunk(c, carry):
        start = pl.multiple_of(c * 32, 32)
        for g in range(4):
            rows = pl.ds(start + 8 * g, 8)
            near[rows, :] = jnp.zeros((8, 128), F32) if before is None else before[rows, :]
        for dz in (-1, 0, 1):
            for n, k in enumerate(shifts):
                sums = pair_sums(
                    targets, start, float(dz), sources, squares, n,
                    pl.multiple_of(start + 32 * (1 + dz), 32), 32, k == 4 and dz == 0,
                )
                for g in range(4):
                    rows = pl.ds(start + 8 * g, 8)
                    near[rows, :] = near[rows, :] + sums[g]
        return carry

    lax.fori_loop(0, 4, chunk, 0)


def near_own_kernel(pos, weighted, pick, near, columns, sources, squares, targets):
    near_part((4,), pos, weighted, (), pick, near, None, columns, sources, squares, targets)


def near_x_kernel(
    pos, weighted, x_low, x_high, pick, before, near, columns, sources, squares, targets
):
    near_part(
        (1, 7), pos, weighted, (x_low, x_high), pick, near, before,
        columns, sources, squares, targets,
    )


ROW_STARTS = (0, 49, 98, 138, 178, 218, 267, 316)


def downward_kernel(
    pos, weighted, counts, before, leaf, par, grand, x_low, x_high, y_low, y_high, operators,
    expand, lanes, down_z, spread, near_pick, leaf_pick, small_pick, place_leaf, place_small,
    out,
    weights, staged, small, leaf_high, leaf_low, small_high, small_low, right_high, right_low,
    sums, flat, basis_x, basis_y, basis_z, local, work_a, work_b, work_c, parents, far,
    near, columns, sources, squares, targets, arrivals,
):
    copies = [
        pltpu.make_async_copy(
            operators.at[pl.ds(ROW_STARTS[n], ROW_STARTS[n + 1] - ROW_STARTS[n])],
            weights.at[pl.ds(ROW_STARTS[n], ROW_STARTS[n + 1] - ROW_STARTS[n])],
            arrivals.at[n],
        )
        for n in range(7)
    ]
    for copy in copies:
        copy.start()

    near[...] = before[...]
    stage_columns(columns, pos, weighted, (x_low, x_high), (y_low, y_high))
    stage_sources(columns, near_pick, 0, SIDEWAYS, sources, squares)
    for component in range(3):
        flat[component] = lanes_first(pos[component])
        targets[component] = flat[component] - 0.5

    def unit_steps(unit, chunks, results):
        level = unit // 12
        dz = (level - 1).astype(F32) if isinstance(level, jax.Array) else float(level - 1)
        for c in chunks:
            base = pl.multiple_of(32 * c + 32 * level + 16 * (unit % 2), 16)
            results[c] = [None] * 4
            yield from pair_steps(
                targets, 32 * c, dz, sources, squares, unit % 12 // 2, base, 16, False, results[c]
            )

    staged[...] = jnp.zeros_like(staged)
    small[...] = jnp.zeros_like(small)
    faces = (x_low, x_high, y_low, y_high)
    for z in range(8):
        columns = slice(z * 128, z * 128 + 128)
        staged[0:64, columns] = leaf[pl.ds(z, 64, stride=8), :]
        for n, buffer in enumerate(faces):
            target = 64 + 16 * n
            staged[target : target + 16, columns] = buffer[pl.ds(z, 16, stride=8), :]
        for n, buffer in enumerate((y_low, y_high)):
            for side in range(2):
                target = 128 + 16 * n + 8 * side
                source = FACE + side * CORNER + z
                staged[target : target + 4, columns] = buffer[pl.ds(source, 4, stride=8), :]
    for z in range(4):
        columns = slice(z % 2 * 128, z % 2 * 128 + 128)
        top = z // 2 * 64
        small[top : top + 16, columns] = par[pl.ds(z, 16, stride=4), :]
        for n, buffer in enumerate(faces):
            target = top + 16 + 8 * n
            small[target : target + 8, columns] = buffer[pl.ds(FACE_PAR + z, 8, stride=4), :]
        for n, buffer in enumerate((y_low, y_high)):
            for side in range(2):
                target = top + 48 + 8 * n + 4 * side
                source = FACE + side * CORNER + COR_PAR + z
                small[target : target + 4, columns] = buffer[pl.ds(source, 4, stride=4), :]
    for z in range(2):
        columns = slice(z * 128, z * 128 + 128)
        small[128:132, columns] = grand[pl.ds(z, 4, stride=2), :]
        for n, buffer in enumerate(faces):
            target = 132 + 4 * n
            small[target : target + 4, columns] = buffer[pl.ds(FACE_GRAND + z, 4, stride=2), :]
        for n, buffer in enumerate((y_low, y_high)):
            for side in range(2):
                target = 148 + 8 * n + 4 * side
                source = FACE + side * CORNER + COR_GRAND + z
                small[target : target + 4, columns] = buffer[pl.ds(source, 4, stride=2), :]

    blank = jnp.zeros((36, 16, 256), BF16)
    for target in (leaf_high, leaf_low):
        target[:, 0] = blank
        target[:, 5] = blank
    for zp in range(4):
        pieces = split2(staged[:, zp * 256 : zp * 256 + 256])
        for piece, target in zip(pieces, (leaf_high, leaf_low)):
            target[:, zp + 1] = mm(leaf_pick[...], piece).astype(BF16).reshape(36, 16, 256)
    for piece, target in zip(split2(small[...]), (small_high, small_low)):
        target[...] = mm(small_pick[...], piece).astype(BF16).reshape(36, 3, 16, 256)

    sums[...] = jnp.zeros_like(sums)

    def left(high, v, d):
        main, rest = (leaf_high, small_high) if high else (leaf_low, small_low)
        return jnp.concatenate(
            [main[v, pl.ds(d, 4)].reshape(64, 256), rest[v, d]], axis=0
        )

    def translate(dx, dy, xs, ys, base, beside, unit, chunks):
        split = {}
        for n, dz in enumerate((-3, -2, 2, 3) if beside else range(-3, 4)):
            split[dz] = split2(weights[base + n])
        none = jnp.zeros((128, 128), BF16)
        right = {}
        for d in range(3):
            for which in range(2):
                right[d, which] = jnp.concatenate(
                    [
                        jnp.concatenate(
                            [
                                split[2 * (d - 1) + source - side][which]
                                if 2 * (d - 1) + source - side in split
                                else none
                                for side in range(2)
                            ],
                            axis=1,
                        )
                        for source in range(2)
                    ],
                    axis=0,
                )
        pass
        sides = [(px, py) for px in xs for py in ys]
        variants = [(px + dx + 2) * 6 + (py + dy + 2) for px, py in sides]
        jobs = []
        for d in (0, 2) if beside else (0, 1, 2):
            upper = jnp.concatenate([left(True, v, d) for v in variants], axis=0)
            lower = jnp.concatenate([left(False, v, d) for v in variants], axis=0)
            jobs += [(jnp.concatenate([upper, lower], axis=0), right[d, 0]), (upper, right[d, 1])]
        results = {}
        steps = unit_steps(unit, chunks, results)
        todo = 16 * len(chunks)
        done = 0
        total = None
        size = 80 * len(sides)
        for n, (a, b) in enumerate(jobs):
            term = mm(a, b)
            if a.shape[0] > size:
                term = term[:size] + term[size:]
            total = term if total is None else total + term
            while done < todo * (n + 1) // len(jobs):
                next(steps)
                done += 1
        for n, (px, py) in enumerate(sides):
            sums[px * 2 + py] = sums[px * 2 + py] + total[n * 80 : n * 80 + 80, :]
        for c in chunks:
            for g in range(4):
                rows = slice(32 * c + 8 * g, 32 * c + 8 * g + 8)
                near[rows, :] = near[rows, :] + results[c][g]

    both = (0, 1)
    every = (0, 1, 2, 3)
    unit = 0
    for n, dx in enumerate(range(-3, 4)):
        copies[n].wait()
        start = ROW_STARTS[n]
        xs = (1,) if dx == -3 else (0,) if dx == 3 else both
        middle = abs(dx) <= 1
        outer = abs(dx) == 3
        low, high = ((0,), (1,)) if dx == -3 else ((2,), (3,)) if dx == 3 else ((0, 1), (2, 3))
        row = 35 if outer else 30 + dx + 2
        translate(dx, -3, xs, (1,), start, False, row, low)
        if middle:
            translate(dx, -2, xs, both, start + 7, False, unit, every)

            def step(i, carry, dx=dx, xs=xs, start=start):
                place = 16 + 3 * (dx + 1) + i
                translate(dx, i - 1, xs, both, start + 14 + 4 * i, True, place, every)
                return carry

            lax.fori_loop(0, 3, step, 0)
            translate(dx, 2, xs, both, start + 26, False, unit + 1, every)
            unit += 2
            last = start + 33
        else:
            chunks = ((0, 1) if dx < 0 else (2, 3)) if outer else every

            def step(i, carry, dx=dx, xs=xs, start=start, unit=unit, chunks=chunks, outer=outer):
                place = 25 + i if outer else unit + i
                translate(dx, i - 2, xs, both, start + 7 + 7 * i, False, place, chunks)
                return carry

            lax.fori_loop(0, 5, step, 0)
            unit += 0 if outer else 5
            last = start + 42
        translate(dx, 3, xs, (0,), last, False, row, high)

    grow, grow_low = split2(expand[...].T)
    grow_both = jnp.concatenate([grow, grow_low], axis=1)
    pairs = [(px, py) for px in both for py in both]

    def expanded(parts):
        placed = [[mm(piece, place).astype(BF16) for piece in split2(rows.T)] for rows, place in parts]
        high = jnp.concatenate([p[0] for p in placed], axis=1)
        low = jnp.concatenate([p[1] for p in placed], axis=1)
        return mm(grow_both, jnp.concatenate([high, high], axis=0)) + mm(grow, low)

    pieces = []
    for q in range(2):
        for z in range(2):
            for px, py in pairs:
                rows = slice(64 + 4 * z, 68 + 4 * z)
                pieces.append(sums[px * 2 + py, rows, q * 128 : q * 128 + 128] * 0.5)
    for px, py in pairs:
        for z in range(2):
            pieces.append(sums[px * 2 + py, 72:73, z * 128 : z * 128 + 128] * 0.25)
    pieces.append(jnp.zeros((56, 128), F32))
    coarse = jnp.concatenate(pieces, axis=0)
    step = split2(down_z[...])

    def share(value, source, low, high):
        for block in range(4):
            rows = slice(block * 128, block * 128 + 128)
            carried = mm3(step, split2(source[rows, :]))
            low[rows, :] = value[rows, 0:128] + carried[0:128]
            high[rows, :] = value[rows, 128:256] + carried[128:256]

    work_a[...] = expanded([(coarse, place_small[2])])
    mix_x(work_a, work_b, lanes, 2, False)
    mix_y(work_b, work_c, lanes, 3, False)
    share(
        expanded([(coarse, place_small[0]), (coarse, place_small[1])]),
        work_c, parents.at[0], parents.at[1],
    )
    for q in range(2):
        mix_x(parents.at[q], work_b, lanes, 0, False)
        mix_y(work_b, work_a, lanes, 1, False)
        parts = []
        for cz in range(2):
            rows = [
                sums[px * 2 + py, (q + 2 * z) * 16 : (q + 2 * z) * 16 + 16, cz * 128 : cz * 128 + 128]
                for z in range(2)
                for px, py in pairs
            ]
            parts.append((jnp.concatenate(rows, axis=0), place_leaf[...]))
        share(expanded(parts), work_a, local.at[2 * q], local.at[2 * q + 1])

    def chunk(c, carry):
        start = pl.multiple_of(c * 32, 32)
        rows = pl.ds(start, 32)
        for a, value in enumerate(basis(flat[0, rows, :])):
            basis_x[a * 32 : a * 32 + 32, :] = value
        for a, value in enumerate(basis(flat[1, rows, :])):
            basis_y[a * 32 : a * 32 + 32, :] = value
        for a, value in enumerate(basis(flat[2, rows, :])):
            basis_z[pl.ds(a, 32, stride=8), :] = value

        def slots(n, carry):
            first = 2 * n
            totals = [None, None]
            along_y = [[bcast(basis_y, b * 32 + first + j) for b in range(8)] for j in range(2)]
            for a in range(8):
                inner = [None, None]
                for b in range(8):
                    value = local[c, (a * 8 + b) * 8 : (a * 8 + b) * 8 + 8, :]
                    for j in range(2):
                        term = value * along_y[j][b]
                        inner[j] = term if inner[j] is None else inner[j] + term
                for j in range(2):
                    term = inner[j] * bcast(basis_x, a * 32 + first + j)
                    totals[j] = term if totals[j] is None else totals[j] + term
            for j in range(2):
                along_z = basis_z[pl.ds(pl.multiple_of((first + j) * 8, 8), 8), :]
                far[pl.ds(start + first + j, 1), :] = jnp.sum(
                    totals[j] * along_z, axis=0, keepdims=True
                )
            return carry

        lax.fori_loop(0, 16, slots, 0, unroll=2)
        return carry

    lax.fori_loop(0, 4, chunk, 0)
    total = (far[...] + near[...]).T
    occupied = occupied_slots(counts, spread)
    out[...] = jnp.concatenate([total[0:64, :], total[64:128, :]], axis=1) * occupied


def vmem(count):
    return [pl.BlockSpec(memory_space=pltpu.VMEM) for _ in range(count)]


def shaped(*dims):
    return jax.ShapeDtypeStruct(dims, F32)


def neighbours(low, high, axis):
    count = lax.axis_size(axis)
    up = [(i, i + 1) for i in range(count - 1)]
    down = [(target, source) for source, target in up]
    return lax.ppermute(high, axis, up), lax.ppermute(low, axis, down)


def per_device(positions, charges, counts, compress, operators, expand):
    const = {name: jnp.asarray(value) for name, value in make_constants().items()}
    pos = positions.reshape(3, 64, 256)
    cells = counts.reshape(64, 8)
    limit = pltpu.CompilerParams(vmem_limit_bytes=56 * 1024 * 1024)
    leaf, par, grand, xs_low, xs_high, ys_low, ys_high, weighted = pl.pallas_call(
        upward_kernel,
        out_shape=[
            shaped(512, 128), shaped(64, 128), shaped(8, 128),
            shaped(PACKED, 128), shaped(PACKED, 128), shaped(FACE, 128), shaped(FACE, 128),
            shaped(64, 256),
        ],
        in_specs=vmem(9),
        out_specs=vmem(8),
        scratch_shapes=[
            pltpu.VMEM((4, 128, 128), F32),
            pltpu.VMEM((256, 128), F32),
            pltpu.VMEM((256, 128), F32),
            pltpu.VMEM((256, 128), F32),
            pltpu.VMEM((4, 512, 128), F32),
            pltpu.VMEM((512, 128), F32),
            pltpu.VMEM((512, 128), F32),
            pltpu.VMEM((2, 512, 128), F32),
        ],
        compiler_params=limit,
        name="upward",
    )(
        pos, charges.reshape(64, 256), cells, compress, const["lanes"], const["up_z"],
        const["pick_par"], const["pick_grand"], const["spread"],
    )
    x_low, x_high = neighbours(xs_low, xs_high, "gx")
    def near_scratch(count):
        return [
            pltpu.VMEM((8, 128, 128), F32),
            pltpu.VMEM((4, count, 192, 128), F32),
            pltpu.VMEM((count, 192, 128), F32),
            pltpu.VMEM((3, 128, 128), F32),
        ]

    near_own = pl.pallas_call(
        near_own_kernel,
        out_shape=shaped(128, 128),
        in_specs=vmem(3),
        out_specs=vmem(1)[0],
        scratch_shapes=near_scratch(1),
        compiler_params=limit,
        cost_estimate=pl.CostEstimate(flops=10**7, bytes_accessed=10**7, transcendentals=0),
        name="near_own",
    )(pos, weighted, const["near_pick"])
    near_own, x_low, x_high = lax.optimization_barrier((near_own, x_low, x_high))
    first, second = slice(FACE, FACE + CORNER), slice(FACE + CORNER, PACKED)
    y_low, y_high = neighbours(
        jnp.concatenate([ys_low, x_low[first], x_high[first]], axis=0),
        jnp.concatenate([ys_high, x_low[second], x_high[second]], axis=0),
        "gy",
    )
    near = pl.pallas_call(
        near_x_kernel,
        out_shape=shaped(128, 128),
        in_specs=vmem(6),
        out_specs=vmem(1)[0],
        scratch_shapes=near_scratch(2),
        compiler_params=limit,
        cost_estimate=pl.CostEstimate(flops=2 * 10**7, bytes_accessed=2 * 10**7, transcendentals=0),
        name="near_x",
    )(pos, weighted, x_low, x_high, const["near_pick"], near_own)
    result = pl.pallas_call(
        downward_kernel,
        out_shape=shaped(64, 256),
        in_specs=vmem(11) + [pl.BlockSpec(memory_space=pl.ANY)] + vmem(9),
        out_specs=vmem(1)[0],
        scratch_shapes=[
            pltpu.VMEM((316, 128, 128), F32),
            pltpu.VMEM((256, 1024), F32),
            pltpu.VMEM((256, 256), F32),
            pltpu.VMEM((36, 6, 16, 256), BF16),
            pltpu.VMEM((36, 6, 16, 256), BF16),
            pltpu.VMEM((36, 3, 16, 256), BF16),
            pltpu.VMEM((36, 3, 16, 256), BF16),
            pltpu.VMEM((3, 256, 256), BF16),
            pltpu.VMEM((3, 256, 256), BF16),
            pltpu.VMEM((4, 80, 256), F32),
            pltpu.VMEM((3, 128, 128), F32),
            pltpu.VMEM((256, 128), F32),
            pltpu.VMEM((256, 128), F32),
            pltpu.VMEM((256, 128), F32),
            pltpu.VMEM((4, 512, 128), F32),
            pltpu.VMEM((512, 128), F32),
            pltpu.VMEM((512, 128), F32),
            pltpu.VMEM((512, 128), F32),
            pltpu.VMEM((2, 512, 128), F32),
            pltpu.VMEM((128, 128), F32),
            pltpu.VMEM((128, 128), F32),
            *near_scratch(6),
            pltpu.SemaphoreType.DMA((7,)),
        ],
        compiler_params=limit,
        name="downward",
    )(
        pos, weighted, cells, near, leaf, par, grand, x_low, x_high, y_low, y_high, operators, expand,
        const["lanes"], const["down_z"], const["spread"], const["near_pick"], const["leaf_pick"],
        const["small_pick"], const["place_leaf"], const["place_small"],
    )
    return result.reshape(8, 8, 256)


def solution(mesh):
    placed = (P(None, "gx", "gy", None), P("gx", "gy", None), P("gx", "gy", None), P(), P(), P())
    return jax.shard_map(
        per_device, mesh=mesh, in_specs=placed, out_specs=P("gx", "gy", None), check_vma=False
    )
```

```python
import math

import jax
import jax.numpy as jnp
import numpy as np
from jax import lax
from jax.experimental import pallas as pl
from jax.experimental.pallas import tpu as pltpu
from jax.sharding import PartitionSpec as P

F32 = jnp.float32
BF16 = jnp.bfloat16
SOFTENING = 0.01
EXACT = lax.Precision.HIGHEST

FACE = 232
CORNER = 64
PACKED = FACE + 2 * CORNER
FACE_PAR, FACE_GRAND, FACE_NEAR = 128, 160, 168
COR_PAR, COR_GRAND, COR_NEAR = 32, 48, 56


SIDEWAYS = (0, 2, 3, 5, 6, 8)


def node_cos():
    return np.array(
        [[math.cos(math.pi * k * (2 * a + 1) / 16) for a in range(8)] for k in range(8)]
    )


def cheb_numpy(points):
    series = np.cos(np.arange(1, 8)[:, None] * np.arccos(points)[None, :])
    return 1 / 8 + 2 / 8 * node_cos()[1:].T @ series


def transfer_factor():
    nodes = np.cos(np.pi * (2 * np.arange(8) + 1) / 16)
    points = 0.5 * (nodes[None, :] + np.array([-1.0, 1.0])[:, None])
    weights = cheb_numpy(points.reshape(-1)).reshape(8, 2, 8)
    return weights.transpose(1, 2, 0)


def make_constants():
    factor = transfer_factor()
    lane = np.arange(128)
    lane_z, lane_x, lane_y = lane // 64, lane // 8 % 8, lane % 8
    lanes = np.zeros((4, 64, 128))
    for level in range(2):
        for which, coordinate in ((0, lane_x), (1, lane_y)):
            side = coordinate >> level & 1
            lanes[2 * level + which] = factor[side].transpose(1, 2, 0).reshape(64, 128)
    up_z = np.zeros((16, 8, 2, 16, 8))
    for block in range(16):
        for side in range(2):
            up_z[block, :, side, block, :] = factor[side].T
    up_z = up_z.reshape(128, 256)
    pick_par = np.zeros((64, 256))
    for x in range(4):
        for y in range(4):
            for z in range(4):
                pick_par[(x * 4 + y) * 4 + z, z % 2 * 128 + z // 2 * 64 + 2 * x * 8 + 2 * y] = 1
    pick_grand = np.zeros((8, 128))
    for x in range(2):
        for y in range(2):
            for z in range(2):
                pick_grand[(x * 2 + y) * 2 + z, z * 64 + 4 * x * 8 + 4 * y] = 1
    spread = np.kron(np.eye(8), np.ones((1, 32)))

    near_row = {}
    for x in range(8):
        for y in range(8):
            near_row[x, y] = x * 8 + y
    for y in range(8):
        near_row[-1, y] = 64 + y
        near_row[8, y] = 72 + y
        near_row[y, -1] = 80 + y
        near_row[y, 8] = 88 + y
    near_row[-1, -1], near_row[8, -1], near_row[-1, 8], near_row[8, 8] = 96, 97, 98, 99
    near_pick = np.zeros((256, 9, 128))
    for k in range(9):
        dx, dy = k // 3 - 1, k % 3 - 1
        for ln in range(128):
            row = near_row[int(lane_x[ln]) + dx, int(lane_y[ln]) + dy]
            near_pick[lane_z[ln] * 128 + row, k, ln] = 1
    near_pick = near_pick[:, SIDEWAYS + (1, 7, 4)].reshape(256, 1152)

    leaf_row = {}
    for x in range(8):
        for y in range(8):
            leaf_row[x, y] = x * 8 + y
    for i in range(2):
        for y in range(8):
            leaf_row[i - 2, y] = 64 + i * 8 + y
            leaf_row[8 + i, y] = 80 + i * 8 + y
            leaf_row[y, i - 2] = 96 + y * 2 + i
            leaf_row[y, 8 + i] = 112 + y * 2 + i
        for j in range(2):
            leaf_row[i - 2, j - 2] = 128 + i * 2 + j
            leaf_row[8 + i, j - 2] = 136 + i * 2 + j
            leaf_row[i - 2, 8 + j] = 144 + i * 2 + j
            leaf_row[8 + i, 8 + j] = 152 + i * 2 + j
    leaf_pick = np.zeros((36, 16, 256))
    for v in range(36):
        sx, sy = v // 6 - 2, v % 6 - 2
        for r in range(16):
            leaf_pick[v, r, leaf_row[2 * (r // 4) + sx, 2 * (r % 4) + sy]] = 1
    leaf_pick = leaf_pick.reshape(576, 256)

    par_row = {}
    for x in range(4):
        for y in range(4):
            par_row[x, y] = x * 4 + y
    for i in range(2):
        for y in range(4):
            par_row[i - 2, y] = 16 + i * 4 + y
            par_row[4 + i, y] = 24 + i * 4 + y
            par_row[y, i - 2] = 32 + y * 2 + i
            par_row[y, 4 + i] = 40 + y * 2 + i
        for j in range(2):
            par_row[i - 2, j - 2] = 48 + i * 2 + j
            par_row[4 + i, j - 2] = 52 + i * 2 + j
            par_row[i - 2, 4 + j] = 56 + i * 2 + j
            par_row[4 + i, 4 + j] = 60 + i * 2 + j
    grand_row = {}
    order = [(0, 0), (-2, 0), (2, 0), (0, -2), (0, 2), (-2, -2), (2, -2), (-2, 2), (2, 2)]
    for n, (ox, oy) in enumerate(order):
        for i in range(2):
            for j in range(2):
                grand_row[ox + i, oy + j] = 128 + n * 4 + i * 2 + j
    small_pick = np.zeros((36, 3, 16, 256))
    for v in range(36):
        sx, sy = v // 6 - 2, v % 6 - 2
        for d in range(3):
            for r in range(8):
                zp = r // 4 + d - 1
                if 0 <= zp < 2:
                    row = par_row[2 * (r // 2 % 2) + sx, 2 * (r % 2) + sy]
                    small_pick[v, d, r, zp * 64 + row] = 1
            if d == 1:
                small_pick[v, d, 8, grand_row[sx, sy]] = 1
    small_pick = small_pick.reshape(1728, 256)

    place_leaf = np.zeros((128, 128))
    for z in range(2):
        for px in range(2):
            for py in range(2):
                for xp in range(4):
                    for yp in range(4):
                        row = ((z * 2 + px) * 2 + py) * 16 + xp * 4 + yp
                        place_leaf[row, z * 64 + (2 * xp + px) * 8 + 2 * yp + py] = 1
    place_small = np.zeros((3, 128, 128))
    for ln in range(128):
        z, x, y = int(lane_z[ln]), int(lane_x[ln]) >> 1, int(lane_y[ln]) >> 1
        for q in range(2):
            row = (((q * 2 + z) * 2 + x % 2) * 2 + y % 2) * 4 + x // 2 * 2 + y // 2
            place_small[q, row, ln] = 1
        place_small[2, 64 + ((x >> 1) * 2 + (y >> 1)) * 2 + z, ln] = 1

    def half(array):
        return np.asarray(array, np.float32).astype(jnp.bfloat16)

    return dict(
        lanes=np.asarray(lanes, np.float32),
        up_z=np.asarray(up_z, np.float32),
        down_z=np.asarray(up_z.T, np.float32),
        pick_par=np.asarray(pick_par, np.float32),
        pick_grand=np.asarray(pick_grand, np.float32),
        spread=half(spread),
        pick_side=half(near_pick[:, :768]),
        pick_x=half(near_pick[:, 768:1024]),
        pick_own=half(near_pick[:, 1024:]),
        leaf_pick=half(leaf_pick),
        small_pick=half(small_pick),
        place_leaf=half(place_leaf),
        place_small=half(place_small),
    )


def mm(a, b):
    return jnp.dot(a, b, preferred_element_type=F32)


def split2(x):
    high = x.astype(BF16)
    return high, (x - high.astype(F32)).astype(BF16)


def split3(x):
    high = x.astype(BF16)
    rest = x - high.astype(F32)
    mid = rest.astype(BF16)
    return high, mid, (rest - mid.astype(F32)).astype(BF16)


def mm3(a, b):
    a_high, a_low = a
    b_high, b_low = b
    return mm(a_high, b_high) + (mm(a_high, b_low) + mm(a_low, b_high))


def lanes_first(block):
    return jnp.concatenate([block[:, :128], block[:, 128:]], axis=0).T


def basis(points):
    u = jnp.clip(2.0 * points - 1.0, -1.0, 1.0)
    series = [None, u]
    for _ in range(2, 8):
        before = series[-2] if len(series) > 2 else 1.0
        series.append(2.0 * u * series[-1] - before)
    table = node_cos()
    weights = [None] * 8
    for a in range(4):
        even = 0.125
        odd = None
        for k in range(1, 8):
            term = series[k] * np.float32(0.25 * table[k, a])
            if k % 2 == 0:
                even = even + term
            else:
                odd = term if odd is None else odd + term
        weights[a] = even + odd
        weights[7 - a] = even - odd
    return weights


def occupied_slots(counts_ref, spread_ref):
    limits = mm(counts_ref[...].astype(F32).astype(BF16), spread_ref[...])
    slot = lax.broadcasted_iota(jnp.int32, (64, 256), 1) & 31
    return jnp.where(slot.astype(F32) < limits, 1.0, 0.0)


def bcast(ref, row):
    return jnp.broadcast_to(ref[pl.ds(row, 1), :], (8, 128))


def mix_x(source, target, lanes_ref, which, up):
    for out in range(8):
        total = None
        for inner in range(8):
            row = inner * 8 + out if up else out * 8 + inner
            term = lanes_ref[which, row : row + 1, :] * source[inner * 64 : inner * 64 + 64, :]
            total = term if total is None else total + term
        if up:
            shift = 8 << (which // 2)
            total = total + pltpu.roll(total, 128 - shift, 1)
        target[out * 64 : out * 64 + 64, :] = total


def mix_y(source, target, lanes_ref, which, up):
    def one(a, carry):
        start = pl.multiple_of(a * 64, 64)
        rows = [source[pl.ds(start + 8 * b, 8), :] for b in range(8)]
        for out in range(8):
            total = None
            for inner in range(8):
                row = inner * 8 + out if up else out * 8 + inner
                term = lanes_ref[which, row : row + 1, :] * rows[inner]
                total = term if total is None else total + term
            if up:
                shift = 1 << (which // 2)
                total = total + pltpu.roll(total, 128 - shift, 1)
            target[pl.ds(start + 8 * out, 8), :] = total
        return carry

    lax.fori_loop(0, 8, one, 0)


def upward_kernel(
    pos, charges, counts, compress, lanes, up_z, pick_par, pick_grand, spread,
    leaf, par, grand, xs_low, xs_high, ys_low, ys_high, weighted,
    flat, basis_x, basis_y, basis_z, moments, work_a, work_b, parents,
):
    w = charges[...] * occupied_slots(counts, spread)
    weighted[...] = w
    for component in range(3):
        flat[component] = lanes_first(pos[component])
    flat[3] = lanes_first(w)

    def chunk(c, carry):
        rows = pl.ds(pl.multiple_of(c * 32, 32), 32)
        mass = flat[3, rows, :]
        for a, value in enumerate(basis(flat[0, rows, :])):
            basis_x[a * 32 : a * 32 + 32, :] = value
        for a, value in enumerate(basis(flat[1, rows, :])):
            basis_y[a * 32 : a * 32 + 32, :] = value * mass
        for a, value in enumerate(basis(flat[2, rows, :])):
            basis_z[pl.ds(a, 32, stride=8), :] = value
        for half in range(2):

            def slot(s, sums):
                along_z = basis_z[pl.ds(pl.multiple_of(s * 8, 8), 8), :]
                along_y = [bcast(basis_y, b * 32 + s) for b in range(8)]
                result = []
                for a in range(4):
                    part = bcast(basis_x, (half * 4 + a) * 32 + s) * along_z
                    for b in range(8):
                        result.append(sums[a * 8 + b] + part * along_y[b])
                return tuple(result)

            zero = jnp.zeros((8, 128), F32)
            sums = lax.fori_loop(0, 32, slot, (zero,) * 32, unroll=16)
            for n in range(32):
                moments[c, (half * 32 + n) * 8 : (half * 32 + n) * 8 + 8, :] = sums[n]
        return carry

    lax.fori_loop(0, 4, chunk, 0)
    compress_t = split2(compress[...].T)
    for first in (0, 2):
        pair = jnp.concatenate([moments[first], moments[first + 1]], axis=1)
        small = mm3(compress_t, split2(pair)).T
        for c in (first, first + 1):
            for z in range(2):
                top = (c - first) * 128 + z * 64
                leaf[pl.ds(c + 4 * z, 64, stride=8), :] = small[top : top + 64, :]

    step = split2(up_z[...])
    for block in range(4):
        rows = slice(block * 128, block * 128 + 128)
        pair = jnp.concatenate(
            [
                jnp.concatenate([moments[cz, rows, :], moments[2 + cz, rows, :]], axis=1)
                for cz in range(2)
            ],
            axis=0,
        )
        joined = mm3(step, split2(pair))
        for q in range(2):
            parents[q, rows, :] = joined[:, 128 * q : 128 * q + 128]
    for q in range(2):
        mix_x(parents.at[q], work_b, lanes, 0, True)
        mix_y(work_b, parents.at[q], lanes, 1, True)
    rough = mm3(compress_t, split2(jnp.concatenate([parents[0], parents[1]], axis=1))).T
    par[...] = jnp.dot(pick_par[...], rough, precision=EXACT, preferred_element_type=F32)
    for block in range(4):
        rows = slice(block * 128, block * 128 + 128)
        pair = jnp.concatenate([parents[0, rows, :], parents[1, rows, :]], axis=0)
        work_a[rows, :] = mm3(step, split2(pair))
    mix_x(work_a, work_b, lanes, 2, True)
    mix_y(work_b, work_a, lanes, 3, True)
    rough = mm3(compress_t, split2(work_a[...])).T
    grand[...] = jnp.dot(pick_grand[...], rough, precision=EXACT, preferred_element_type=F32)

    def particle(component, cells, part):
        columns = slice(part * 128, part * 128 + 128)
        if component < 3:
            return pos[component, cells, columns]
        return weighted[cells, columns]

    for buffer, x0, px0, xn in ((xs_low, 0, 0, 0), (xs_high, 6, 2, 7)):
        buffer[0:128, :] = leaf[x0 * 64 : x0 * 64 + 128, :]
        buffer[FACE_PAR : FACE_PAR + 32, :] = par[px0 * 16 : px0 * 16 + 32, :]
        buffer[FACE_GRAND : FACE_GRAND + 8, :] = grand[...]
        for corner, y0, py0, yn in ((FACE, 0, 0, 0), (FACE + CORNER, 6, 2, 7)):
            for i in range(2):
                source = ((x0 + i) * 8 + y0) * 8
                buffer[corner + i * 16 : corner + i * 16 + 16, :] = leaf[source : source + 16, :]
                source = ((px0 + i) * 4 + py0) * 4
                target = corner + COR_PAR + i * 8
                buffer[target : target + 8, :] = par[source : source + 8, :]
            target = corner + COR_GRAND
            buffer[target : target + 8, :] = grand[...]
        for component in range(4):
            for part in range(2):
                row = 2 * component + part
                value = particle(component, slice(xn * 8, xn * 8 + 8), part)
                buffer[pl.ds(FACE_NEAR + row, 8, stride=8), :] = value
                for corner, yn in ((FACE, 0), (FACE + CORNER, 7)):
                    target = corner + COR_NEAR + row
                    buffer[target : target + 1, :] = value[yn : yn + 1, :]
    for buffer, y0, py0, yn in ((ys_low, 0, 0, 0), (ys_high, 6, 2, 7)):
        for x in range(8):
            source = (x * 8 + y0) * 8
            buffer[x * 16 : x * 16 + 16, :] = leaf[source : source + 16, :]
        for x in range(4):
            source = (x * 4 + py0) * 4
            target = FACE_PAR + x * 8
            buffer[target : target + 8, :] = par[source : source + 8, :]
        buffer[FACE_GRAND : FACE_GRAND + 8, :] = grand[...]
        for x in range(8):
            for component in range(4):
                for part in range(2):
                    value = particle(component, slice(x * 8 + yn, x * 8 + yn + 1), part)
                    target = FACE_NEAR + x * 8 + 2 * component + part
                    buffer[target : target + 1, :] = value


def stage_columns(columns, pos, weighted, x_faces, y_faces):
    columns[...] = jnp.zeros_like(columns)
    for component in range(4):
        for part in range(2):
            row = 2 * component + part
            lanes = slice(part * 128, part * 128 + 128)
            own = pos[component, :, lanes] if component < 3 else weighted[:, lanes]
            columns[row, 0:64, :] = own
            for n, buffer in enumerate((*x_faces, *y_faces)):
                columns[row, 64 + 8 * n : 72 + 8 * n, :] = buffer[
                    pl.ds(FACE_NEAR + row, 8, stride=8), :
                ]
            for n, buffer in enumerate(y_faces):
                for side in range(2):
                    source = FACE + side * CORNER + COR_NEAR + row
                    target = 96 + 2 * n + side
                    columns[row, target : target + 1, :] = buffer[source : source + 1, :]


def stage_sources(columns, pick, shifts, sources, squares):
    empty = jnp.zeros((32, 128), F32)
    for component in range(4):
        low = columns[2 * component].T
        high = columns[2 * component + 1].T
        left = jnp.concatenate([empty, low, high[0:32, :]], axis=0)
        right = jnp.concatenate([low[96:128, :], high, empty], axis=0)
        pieces = jnp.concatenate(split3(jnp.concatenate([left, right], axis=1)), axis=0)
        for first in range(0, len(shifts), 2):
            width = 128 * min(2, len(shifts) - first)
            chosen = mm(pieces, pick[:, 128 * first : 128 * first + width])
            chosen = (chosen[0:192] + chosen[192:384]) + chosen[384:576]
            for n in range(first, first + width // 128):
                value = chosen[:, 128 * (n - first) : 128 * (n - first) + 128]
                if component == 3:
                    sources[3, n] = value
                    continue
                offset = (shifts[n] // 3 - 1, shifts[n] % 3 - 1, 0)[component] - 0.5
                value = value + offset
                sources[component, n] = -2.0 * value
                if component == 0:
                    squares[n] = value * value + SOFTENING
                else:
                    squares[n] = squares[n] + value * value


def pair_steps(targets, start, dz, sources, squares, n, base, count, own, sums):
    groups = [
        [targets[component, pl.ds(start + 8 * g, 8), :] for component in range(3)]
        for g in range(4)
    ]
    high = [t[2] - dz for t in groups]
    square = [t[0] * t[0] + t[1] * t[1] + h * h for t, h in zip(groups, high)]
    slot = lax.broadcasted_iota(jnp.int32, (8, 128), 0)
    for s in range(count):
        row = pl.ds(base + s, 1)
        px = jnp.broadcast_to(sources[0, n, row, :], (8, 128))
        py = jnp.broadcast_to(sources[1, n, row, :], (8, 128))
        pz = jnp.broadcast_to(sources[2, n, row, :], (8, 128))
        pw = jnp.broadcast_to(sources[3, n, row, :], (8, 128))
        pq = jnp.broadcast_to(squares[n, row, :], (8, 128))
        for g in range(4):
            distance = (square[g] + pq) + groups[g][0] * px + (groups[g][1] * py + high[g] * pz)
            term = pw * lax.rsqrt(distance)
            if own and s // 8 == g:
                term = jnp.where(slot == s % 8, 0.0, term)
            sums[g] = term if sums[g] is None else sums[g] + term
        yield


def pair_sums(*arguments):
    sums = [None] * 4
    for _ in pair_steps(*arguments, sums):
        pass
    return sums


def near_part(shifts, pos, weighted, x_faces, pick, near, before, columns, sources, squares, targets):
    stage_columns(columns, pos, weighted, x_faces, ())
    stage_sources(columns, pick, shifts, sources, squares)
    for component in range(3):
        targets[component] = lanes_first(pos[component]) - 0.5

    def chunk(c, carry):
        start = pl.multiple_of(c * 32, 32)
        for g in range(4):
            rows = pl.ds(start + 8 * g, 8)
            near[rows, :] = jnp.zeros((8, 128), F32) if before is None else before[rows, :]
        for dz in (-1, 0, 1):
            for n, k in enumerate(shifts):
                sums = pair_sums(
                    targets, start, float(dz), sources, squares, n,
                    pl.multiple_of(start + 32 * (1 + dz), 32), 32, k == 4 and dz == 0,
                )
                for g in range(4):
                    rows = pl.ds(start + 8 * g, 8)
                    near[rows, :] = near[rows, :] + sums[g]
        return carry

    lax.fori_loop(0, 4, chunk, 0)


def near_own_kernel(pos, weighted, pick, near, columns, sources, squares, targets):
    near_part((4,), pos, weighted, (), pick, near, None, columns, sources, squares, targets)


def near_x_kernel(
    pos, weighted, x_low, x_high, pick, before, near, columns, sources, squares, targets
):
    near_part(
        (1, 7), pos, weighted, (x_low, x_high), pick, near, before,
        columns, sources, squares, targets,
    )


ROW_STARTS = (0, 49, 98, 138, 178, 218, 267, 316)


def downward_kernel(
    pos, weighted, counts, before, leaf, par, grand, x_low, x_high, y_low, y_high, operators,
    expand, lanes, down_z, spread, near_pick, leaf_pick, small_pick, place_leaf, place_small,
    out,
    weights, staged, small, leaf_high, leaf_low, small_high, small_low, right_high, right_low,
    sums, flat, basis_x, basis_y, basis_z, local, work_a, work_b, work_c, parents, far,
    near, columns, sources, squares, targets, arrivals,
):
    copies = [
        pltpu.make_async_copy(
            operators.at[pl.ds(ROW_STARTS[n], ROW_STARTS[n + 1] - ROW_STARTS[n])],
            weights.at[pl.ds(ROW_STARTS[n], ROW_STARTS[n + 1] - ROW_STARTS[n])],
            arrivals.at[n],
        )
        for n in range(7)
    ]
    for copy in copies:
        copy.start()

    near[...] = before[...]
    stage_columns(columns, pos, weighted, (x_low, x_high), (y_low, y_high))
    stage_sources(columns, near_pick, SIDEWAYS, sources, squares)
    for component in range(3):
        flat[component] = lanes_first(pos[component])
        targets[component] = flat[component] - 0.5

    def unit_steps(unit, chunks, results):
        level = unit // 12
        dz = (level - 1).astype(F32) if isinstance(level, jax.Array) else float(level - 1)
        for c in chunks:
            base = pl.multiple_of(32 * c + 32 * level + 16 * (unit % 2), 16)
            results[c] = [None] * 4
            yield from pair_steps(
                targets, 32 * c, dz, sources, squares, unit % 12 // 2, base, 16, False, results[c]
            )

    staged[...] = jnp.zeros_like(staged)
    small[...] = jnp.zeros_like(small)
    faces = (x_low, x_high, y_low, y_high)
    for z in range(8):
        columns = slice(z * 128, z * 128 + 128)
        staged[0:64, columns] = leaf[pl.ds(z, 64, stride=8), :]
        for n, buffer in enumerate(faces):
            target = 64 + 16 * n
            staged[target : target + 16, columns] = buffer[pl.ds(z, 16, stride=8), :]
        for n, buffer in enumerate((y_low, y_high)):
            for side in range(2):
                target = 128 + 16 * n + 8 * side
                source = FACE + side * CORNER + z
                staged[target : target + 4, columns] = buffer[pl.ds(source, 4, stride=8), :]
    for z in range(4):
        columns = slice(z % 2 * 128, z % 2 * 128 + 128)
        top = z // 2 * 64
        small[top : top + 16, columns] = par[pl.ds(z, 16, stride=4), :]
        for n, buffer in enumerate(faces):
            target = top + 16 + 8 * n
            small[target : target + 8, columns] = buffer[pl.ds(FACE_PAR + z, 8, stride=4), :]
        for n, buffer in enumerate((y_low, y_high)):
            for side in range(2):
                target = top + 48 + 8 * n + 4 * side
                source = FACE + side * CORNER + COR_PAR + z
                small[target : target + 4, columns] = buffer[pl.ds(source, 4, stride=4), :]
    for z in range(2):
        columns = slice(z * 128, z * 128 + 128)
        small[128:132, columns] = grand[pl.ds(z, 4, stride=2), :]
        for n, buffer in enumerate(faces):
            target = 132 + 4 * n
            small[target : target + 4, columns] = buffer[pl.ds(FACE_GRAND + z, 4, stride=2), :]
        for n, buffer in enumerate((y_low, y_high)):
            for side in range(2):
                target = 148 + 8 * n + 4 * side
                source = FACE + side * CORNER + COR_GRAND + z
                small[target : target + 4, columns] = buffer[pl.ds(source, 4, stride=2), :]

    blank = jnp.zeros((36, 16, 256), BF16)
    for target in (leaf_high, leaf_low):
        target[:, 0] = blank
        target[:, 5] = blank
    for zp in range(4):
        pieces = split2(staged[:, zp * 256 : zp * 256 + 256])
        for piece, target in zip(pieces, (leaf_high, leaf_low)):
            target[:, zp + 1] = mm(leaf_pick[...], piece).astype(BF16).reshape(36, 16, 256)
    for piece, target in zip(split2(small[...]), (small_high, small_low)):
        target[...] = mm(small_pick[...], piece).astype(BF16).reshape(36, 3, 16, 256)

    sums[...] = jnp.zeros_like(sums)

    def left(high, v, d):
        main, rest = (leaf_high, small_high) if high else (leaf_low, small_low)
        return jnp.concatenate(
            [main[v, pl.ds(d, 4)].reshape(64, 256), rest[v, d]], axis=0
        )

    def translate(dx, dy, xs, ys, base, beside, unit, chunks):
        split = {}
        for n, dz in enumerate((-3, -2, 2, 3) if beside else range(-3, 4)):
            split[dz] = split2(weights[base + n])
        none = jnp.zeros((128, 128), BF16)
        right = {}
        for d in range(3):
            for which in range(2):
                right[d, which] = jnp.concatenate(
                    [
                        jnp.concatenate(
                            [
                                split[2 * (d - 1) + source - side][which]
                                if 2 * (d - 1) + source - side in split
                                else none
                                for side in range(2)
                            ],
                            axis=1,
                        )
                        for source in range(2)
                    ],
                    axis=0,
                )
        pass
        sides = [(px, py) for px in xs for py in ys]
        variants = [(px + dx + 2) * 6 + (py + dy + 2) for px, py in sides]
        jobs = []
        for d in (0, 2) if beside else (0, 1, 2):
            upper = jnp.concatenate([left(True, v, d) for v in variants], axis=0)
            lower = jnp.concatenate([left(False, v, d) for v in variants], axis=0)
            jobs += [(jnp.concatenate([upper, lower], axis=0), right[d, 0]), (upper, right[d, 1])]
        results = {}
        steps = unit_steps(unit, chunks, results)
        todo = 16 * len(chunks)
        done = 0
        total = None
        size = 80 * len(sides)
        for n, (a, b) in enumerate(jobs):
            term = mm(a, b)
            if a.shape[0] > size:
                term = term[:size] + term[size:]
            total = term if total is None else total + term
            while done < todo * (n + 1) // len(jobs):
                next(steps)
                done += 1
        for n, (px, py) in enumerate(sides):
            sums[px * 2 + py] = sums[px * 2 + py] + total[n * 80 : n * 80 + 80, :]
        for c in chunks:
            for g in range(4):
                rows = slice(32 * c + 8 * g, 32 * c + 8 * g + 8)
                near[rows, :] = near[rows, :] + results[c][g]

    both = (0, 1)
    every = (0, 1, 2, 3)
    unit = 0
    for n, dx in enumerate(range(-3, 4)):
        copies[n].wait()
        start = ROW_STARTS[n]
        xs = (1,) if dx == -3 else (0,) if dx == 3 else both
        middle = abs(dx) <= 1
        outer = abs(dx) == 3
        low, high = ((0,), (1,)) if dx == -3 else ((2,), (3,)) if dx == 3 else ((0, 1), (2, 3))
        row = 35 if outer else 30 + dx + 2
        translate(dx, -3, xs, (1,), start, False, row, low)
        if middle:
            translate(dx, -2, xs, both, start + 7, False, unit, every)

            def step(i, carry, dx=dx, xs=xs, start=start):
                place = 16 + 3 * (dx + 1) + i
                translate(dx, i - 1, xs, both, start + 14 + 4 * i, True, place, every)
                return carry

            lax.fori_loop(0, 3, step, 0)
            translate(dx, 2, xs, both, start + 26, False, unit + 1, every)
            unit += 2
            last = start + 33
        else:
            chunks = ((0, 1) if dx < 0 else (2, 3)) if outer else every

            def step(i, carry, dx=dx, xs=xs, start=start, unit=unit, chunks=chunks, outer=outer):
                place = 25 + i if outer else unit + i
                translate(dx, i - 2, xs, both, start + 7 + 7 * i, False, place, chunks)
                return carry

            lax.fori_loop(0, 5, step, 0)
            unit += 0 if outer else 5
            last = start + 42
        translate(dx, 3, xs, (0,), last, False, row, high)

    grow, grow_low = split2(expand[...].T)
    grow_both = jnp.concatenate([grow, grow_low], axis=1)
    pairs = [(px, py) for px in both for py in both]

    def expanded(parts):
        placed = [[mm(piece, place).astype(BF16) for piece in split2(rows.T)] for rows, place in parts]
        high = jnp.concatenate([p[0] for p in placed], axis=1)
        low = jnp.concatenate([p[1] for p in placed], axis=1)
        return mm(grow_both, jnp.concatenate([high, high], axis=0)) + mm(grow, low)

    pieces = []
    for q in range(2):
        for z in range(2):
            for px, py in pairs:
                rows = slice(64 + 4 * z, 68 + 4 * z)
                pieces.append(sums[px * 2 + py, rows, q * 128 : q * 128 + 128] * 0.5)
    for px, py in pairs:
        for z in range(2):
            pieces.append(sums[px * 2 + py, 72:73, z * 128 : z * 128 + 128] * 0.25)
    pieces.append(jnp.zeros((56, 128), F32))
    coarse = jnp.concatenate(pieces, axis=0)
    step = split2(down_z[...])

    def share(value, source, low, high):
        for block in range(4):
            rows = slice(block * 128, block * 128 + 128)
            carried = mm3(step, split2(source[rows, :]))
            low[rows, :] = value[rows, 0:128] + carried[0:128]
            high[rows, :] = value[rows, 128:256] + carried[128:256]

    work_a[...] = expanded([(coarse, place_small[2])])
    mix_x(work_a, work_b, lanes, 2, False)
    mix_y(work_b, work_c, lanes, 3, False)
    share(
        expanded([(coarse, place_small[0]), (coarse, place_small[1])]),
        work_c, parents.at[0], parents.at[1],
    )
    for q in range(2):
        mix_x(parents.at[q], work_b, lanes, 0, False)
        mix_y(work_b, work_a, lanes, 1, False)
        parts = []
        for cz in range(2):
            rows = [
                sums[px * 2 + py, (q + 2 * z) * 16 : (q + 2 * z) * 16 + 16, cz * 128 : cz * 128 + 128]
                for z in range(2)
                for px, py in pairs
            ]
            parts.append((jnp.concatenate(rows, axis=0), place_leaf[...]))
        share(expanded(parts), work_a, local.at[2 * q], local.at[2 * q + 1])

    def chunk(c, carry):
        start = pl.multiple_of(c * 32, 32)
        rows = pl.ds(start, 32)
        for a, value in enumerate(basis(flat[0, rows, :])):
            basis_x[a * 32 : a * 32 + 32, :] = value
        for a, value in enumerate(basis(flat[1, rows, :])):
            basis_y[a * 32 : a * 32 + 32, :] = value
        for a, value in enumerate(basis(flat[2, rows, :])):
            basis_z[pl.ds(a, 32, stride=8), :] = value

        def slots(n, carry):
            first = 2 * n
            totals = [None, None]
            along_y = [[bcast(basis_y, b * 32 + first + j) for b in range(8)] for j in range(2)]
            for a in range(8):
                inner = [None, None]
                for b in range(8):
                    value = local[c, (a * 8 + b) * 8 : (a * 8 + b) * 8 + 8, :]
                    for j in range(2):
                        term = value * along_y[j][b]
                        inner[j] = term if inner[j] is None else inner[j] + term
                for j in range(2):
                    term = inner[j] * bcast(basis_x, a * 32 + first + j)
                    totals[j] = term if totals[j] is None else totals[j] + term
            for j in range(2):
                along_z = basis_z[pl.ds(pl.multiple_of((first + j) * 8, 8), 8), :]
                far[pl.ds(start + first + j, 1), :] = jnp.sum(
                    totals[j] * along_z, axis=0, keepdims=True
                )
            return carry

        lax.fori_loop(0, 16, slots, 0, unroll=4)
        return carry

    lax.fori_loop(0, 4, chunk, 0)
    total = (far[...] + near[...]).T
    occupied = occupied_slots(counts, spread)
    out[...] = jnp.concatenate([total[0:64, :], total[64:128, :]], axis=1) * occupied


def vmem(count):
    return [pl.BlockSpec(memory_space=pltpu.VMEM) for _ in range(count)]


def shaped(*dims):
    return jax.ShapeDtypeStruct(dims, F32)


def neighbours(low, high, axis):
    count = lax.axis_size(axis)
    up = [(i, i + 1) for i in range(count - 1)]
    down = [(target, source) for source, target in up]
    return lax.ppermute(high, axis, up), lax.ppermute(low, axis, down)


def per_device(positions, charges, counts, compress, operators, expand):
    const = {name: jnp.asarray(value) for name, value in make_constants().items()}
    pos = positions.reshape(3, 64, 256)
    cells = counts.reshape(64, 8)
    limit = pltpu.CompilerParams(vmem_limit_bytes=56 * 1024 * 1024)
    leaf, par, grand, xs_low, xs_high, ys_low, ys_high, weighted = pl.pallas_call(
        upward_kernel,
        out_shape=[
            shaped(512, 128), shaped(64, 128), shaped(8, 128),
            shaped(PACKED, 128), shaped(PACKED, 128), shaped(FACE, 128), shaped(FACE, 128),
            shaped(64, 256),
        ],
        in_specs=vmem(9),
        out_specs=vmem(8),
        scratch_shapes=[
            pltpu.VMEM((4, 128, 128), F32),
            pltpu.VMEM((256, 128), F32),
            pltpu.VMEM((256, 128), F32),
            pltpu.VMEM((256, 128), F32),
            pltpu.VMEM((4, 512, 128), F32),
            pltpu.VMEM((512, 128), F32),
            pltpu.VMEM((512, 128), F32),
            pltpu.VMEM((2, 512, 128), F32),
        ],
        compiler_params=limit,
        name="upward",
    )(
        pos, charges.reshape(64, 256), cells, compress, const["lanes"], const["up_z"],
        const["pick_par"], const["pick_grand"], const["spread"],
    )
    x_low, x_high = neighbours(xs_low, xs_high, "gx")
    def near_scratch(count):
        return [
            pltpu.VMEM((8, 128, 128), F32),
            pltpu.VMEM((4, count, 192, 128), F32),
            pltpu.VMEM((count, 192, 128), F32),
            pltpu.VMEM((3, 128, 128), F32),
        ]

    near_own = pl.pallas_call(
        near_own_kernel,
        out_shape=shaped(128, 128),
        in_specs=vmem(3),
        out_specs=vmem(1)[0],
        scratch_shapes=near_scratch(1),
        compiler_params=limit,
        cost_estimate=pl.CostEstimate(flops=10**7, bytes_accessed=10**7, transcendentals=0),
        name="near_own",
    )(pos, weighted, const["pick_own"])
    near_own, x_low, x_high = lax.optimization_barrier((near_own, x_low, x_high))
    first, second = slice(FACE, FACE + CORNER), slice(FACE + CORNER, PACKED)
    y_low, y_high = neighbours(
        jnp.concatenate([ys_low, x_low[first], x_high[first]], axis=0),
        jnp.concatenate([ys_high, x_low[second], x_high[second]], axis=0),
        "gy",
    )
    near = pl.pallas_call(
        near_x_kernel,
        out_shape=shaped(128, 128),
        in_specs=vmem(6),
        out_specs=vmem(1)[0],
        scratch_shapes=near_scratch(2),
        compiler_params=limit,
        cost_estimate=pl.CostEstimate(flops=2 * 10**7, bytes_accessed=2 * 10**7, transcendentals=0),
        name="near_x",
    )(pos, weighted, x_low, x_high, const["pick_x"], near_own)
    result = pl.pallas_call(
        downward_kernel,
        out_shape=shaped(64, 256),
        in_specs=vmem(11) + [pl.BlockSpec(memory_space=pl.ANY)] + vmem(9),
        out_specs=vmem(1)[0],
        scratch_shapes=[
            pltpu.VMEM((316, 128, 128), F32),
            pltpu.VMEM((256, 1024), F32),
            pltpu.VMEM((256, 256), F32),
            pltpu.VMEM((36, 6, 16, 256), BF16),
            pltpu.VMEM((36, 6, 16, 256), BF16),
            pltpu.VMEM((36, 3, 16, 256), BF16),
            pltpu.VMEM((36, 3, 16, 256), BF16),
            pltpu.VMEM((3, 256, 256), BF16),
            pltpu.VMEM((3, 256, 256), BF16),
            pltpu.VMEM((4, 80, 256), F32),
            pltpu.VMEM((3, 128, 128), F32),
            pltpu.VMEM((256, 128), F32),
            pltpu.VMEM((256, 128), F32),
            pltpu.VMEM((256, 128), F32),
            pltpu.VMEM((4, 512, 128), F32),
            pltpu.VMEM((512, 128), F32),
            pltpu.VMEM((512, 128), F32),
            pltpu.VMEM((512, 128), F32),
            pltpu.VMEM((2, 512, 128), F32),
            pltpu.VMEM((128, 128), F32),
            pltpu.VMEM((128, 128), F32),
            *near_scratch(6),
            pltpu.SemaphoreType.DMA((7,)),
        ],
        compiler_params=limit,
        name="downward",
    )(
        pos, weighted, cells, near, leaf, par, grand, x_low, x_high, y_low, y_high, operators, expand,
        const["lanes"], const["down_z"], const["spread"], const["pick_side"], const["leaf_pick"],
        const["small_pick"], const["place_leaf"], const["place_small"],
    )
    return result.reshape(8, 8, 256)


def solution(mesh):
    placed = (P(None, "gx", "gy", None), P("gx", "gy", None), P("gx", "gy", None), P(), P(), P())
    return jax.shard_map(
        per_device, mesh=mesh, in_specs=placed, out_specs=P("gx", "gy", None), check_vma=False
    )
```
